256 devices in a mesh: dp: 16 (over x_hi, y, core), vocab: 16 (over z, x_lo).
Axes of the slice: x: 4 (x_hi: 2, x_lo: 2; x = x_hi * 2 + x_lo), y: 4, z: 8, core: 2. Of those that a mesh axis runs over, the one named last changes fastest.
Arguments:
- hidden: bfloat16 [512, 4096], P('dp'), may hold values from -6 to 6
- head_weight: bfloat16 [4096, 98304], P(None, ('dp', 'vocab')), may hold values from -0.09375 to 0.09375
- vocab_bias: float32 [98304], P(('dp', 'vocab')), may hold values from -4.5 to 0
- seq_ids: int32 [16, 32], P('dp'), may hold values from 0 to 3, never falling along the last dimension, each value on 1 to 16 neighbouring positions
- token_mask: int32 [16, 32], P('dp'), may hold values 0 or 1
- labels: int32 [32], replicated, may hold values from 0 to 31
Outputs:
- batch_loss: float32 [], replicated
- weight_grad: bfloat16 [4096, 98304], P(None, ('dp', 'vocab'))
- hidden_grad: float32 [512, 4096], P(('dp', 'vocab'))
The draws below stay inside these ranges and needn't reach their ends.
All inputs are finite; a program needn't handle non-finite values. No bound on the sum of `token_mask` on one device may be relied on, other than what follows from the above.
Results may differ from the reference program's by a relative error of at most 0.011.
Values may be sent and summed in bfloat16 or wider, within the bound.
A program may use at most 128 MiB of HBM per device.

```python
import math
from functools import partial
import jax
import jax.numpy as jnp
import numpy as np
from jax import lax

D = 4096
VOC_DEV = 384
TOK_GROUP = 32
QRY_GROUP = 2
SEQ_GROUP = 4
V = 98304
TOKENS = 512
QUERIES = 32
PASSAGES = 32
N_DP = 16
N_VOCAB = 16


def draw_vocab_bias(key, part):
    key = jax.random.fold_in(key, 11)
    position = jnp.arange(V, dtype=jnp.float32) / V
    jitter = jax.random.uniform(key, (V,), jnp.float32, -0.75, 0.75)
    baseline = -3.5 + 2.5 * position
    return jnp.clip(baseline + jitter, -4.5, 0.0)


def touch_ends(entries, rng, least, high):
    longest = entries.shape.index(max(entries.shape))
    spots = []
    for shift in (0, 1):
        where = [jax.random.randint(jax.random.fold_in(rng, axis), (), 0, length) for axis, length in enumerate(entries.shape)]
        where[longest] = (where[longest] + shift) % entries.shape[longest]
        spots.append(tuple(where))
    return entries.at[spots[0]].set(least).at[spots[1]].set(high)


def levels(stream_key, dims, pieces, low, high):
    gain, own = 1.0, jax.random.fold_in(stream_key, 6)
    for dim, parts in pieces:
        heights = jnp.exp(jax.random.uniform(jax.random.fold_in(own, dim), (parts,), jnp.float32, low / len(pieces), high / len(pieces)))
        gain = gain * jnp.repeat(heights, dims[dim] // parts).reshape([-1 if axis == dim else 1 for axis in range(len(dims))])
    return gain


def split_up(number_of, total, most, lean):
    weights = [(1 << 20) // math.isqrt(rank ** lean) + 1 for rank in range(2, number_of + 1)]
    surplus, given = total - most - (number_of - 1), [1] * (number_of - 1)
    while surplus > 0:
        free = [i for i in range(number_of - 1) if given[i] < most]
        pool, budget = sum([weights[i] for i in free]), surplus
        for i in free:
            more = min(most - given[i], max(1, budget * weights[i] // pool), surplus)
            given[i] = given[i] + more
            surplus = surplus - more
    return np.array([most] + given)


def ragged_sizes(key, amount, total, reach, skew):
    if amount == 2:
        one = jax.random.randint(key, (), max(1, total - reach), min(reach, total - 1) + 1)
        return jnp.stack([one, total - one])
    lengths = jnp.asarray(split_up(amount, total, reach, skew), jnp.int32)
    twos = (amount - 1) // 2
    giver, sink = lengths[1:1 + 2 * twos:2], lengths[2:2 + 2 * twos:2]
    margin = jnp.minimum(giver - 1, reach - sink)
    shifted = jax.random.randint(jax.random.fold_in(key, 1), (twos,), 0, 1 << 20) % (margin + 1)
    lengths = lengths.at[1:1 + 2 * twos:2].set(giver - shifted).at[2:2 + 2 * twos:2].set(sink + shifted)
    return lengths[jax.random.permutation(jax.random.fold_in(key, 2), amount)]


def bell_draw(own_key, shape, scale, most, shards=(), kind=jnp.bfloat16):
    values = scale * jax.random.normal(own_key, shape, jnp.float32)
    if shards:
        values = values * levels(own_key, shape, shards, -0.22, 0.18)
    return jnp.clip(values, -most, most).astype(kind)


def setup_inputs(seed: int = 0) -> dict:
    streams_of = jax.random.split(jax.random.key(seed), 7)
    return {
        "hidden": bell_draw(streams_of[0], (TOKENS, D), 1.0, 6.0, ((0, 16),)),
        "head_weight": bell_draw(streams_of[1], (D, V), D ** -0.5, 0.09375, ((1, 256),)),
        "vocab_bias": draw_vocab_bias(jax.random.fold_in(streams_of[6], 71), 0),
        "seq_ids": jax.vmap(lambda own: jnp.searchsorted(jnp.cumsum(ragged_sizes(own, SEQ_GROUP, TOK_GROUP, TOK_GROUP // 2, 1)), jnp.arange(TOK_GROUP), side="right"))(jax.random.split(streams_of[3], N_DP)).reshape((N_DP, TOK_GROUP)).astype(jnp.int32),
        "token_mask": touch_ends((jax.random.randint(streams_of[4], (N_DP, TOK_GROUP), 0, 8) < 7).astype(jnp.int32), jax.random.fold_in(streams_of[4], 1), 0, 1),
        "labels": touch_ends(jax.random.randint(streams_of[5], (PASSAGES,), 0, QUERIES), jax.random.fold_in(streams_of[5], 1), 0, QUERIES - 1).astype(jnp.int32),
    }


pool_power = 4.0
score_scale = 20.0
loss_scale = 65536.0
norm_eps = 1e-06
precise = lax.Precision.HIGHEST

def pool_tables(seq_tags, mask_tags):
    groups = seq_tags.shape[0]
    seq_total = groups * SEQ_GROUP
    numbers = (seq_tags + SEQ_GROUP * jnp.arange(groups, dtype=jnp.int32)[:, None]).reshape(-1)
    member = (numbers[None, :] == jnp.arange(seq_total, dtype=jnp.int32)[:, None]) & (mask_tags.reshape(-1)[None, :] > 0)
    counts = lax.optimization_barrier(jnp.sum(member.astype(jnp.int32), axis=1))
    return member.astype(jnp.float32) / jnp.maximum(counts, 1).astype(jnp.float32)[:, None]

def split_sequences(pooled):
    groups = pooled.shape[0] // SEQ_GROUP
    shaped = pooled.reshape(groups, SEQ_GROUP, pooled.shape[1])
    return (shaped[:, :QRY_GROUP].reshape(-1, pooled.shape[1]), shaped[:, QRY_GROUP:].reshape(-1, pooled.shape[1]))

def products(former, latter):
    return lax.dot_general(former, latter, (((1,), (1,)), ((), ())), precision=precise, preferred_element_type=jnp.float32)

def batch_objective(pooled_sum, labels):
    pooled = jnp.log1p(pooled_sum) / pool_power
    seq_norms = jnp.sqrt(lax.optimization_barrier(jnp.sum(pooled * pooled, axis=1)) + norm_eps)
    query_vecs, passage_vecs = split_sequences(pooled)
    query_norms, passage_norms = split_sequences(seq_norms[:, None])
    cosine = products(query_vecs, passage_vecs) / (query_norms * passage_norms.T)
    scores = score_scale * cosine
    totals = lax.optimization_barrier(jnp.sum(jnp.exp(scores), axis=0))
    chosen = (jnp.arange(scores.shape[0], dtype=jnp.int32)[:, None] == labels[None, :]).astype(scores.dtype)
    return jnp.mean(jnp.log(totals) - lax.optimization_barrier(jnp.sum(chosen * scores, axis=0)))

def reference(hidden, head_weight, vocab_bias, seq_ids, token_mask, labels):
    pool_weights = pool_tables(seq_ids, token_mask)
    block_size = VOC_DEV * N_VOCAB
    block_count = N_DP
    indices = jnp.arange(block_count, dtype=jnp.int32)

    def block_logits(block_index):
        offset = (block_index * block_size).astype(jnp.int32)
        weight_block = lax.dynamic_slice_in_dim(head_weight, offset, block_size, 1)
        bias_block = lax.dynamic_slice_in_dim(vocab_bias, offset, block_size, 0)
        logits = jnp.dot(hidden, weight_block, preferred_element_type=jnp.float32) + bias_block[None, :]
        return (logits, weight_block)

    def forward(block_index):
        logits, unused_block = block_logits(block_index)
        saturated = jnp.log1p(jax.nn.softplus(logits))
        excess = (1.0 + saturated) ** pool_power - 1.0
        return jnp.dot(pool_weights, excess, precision=precise, preferred_element_type=jnp.float32)
    stacked = lax.map(forward, indices)
    pooled_sum = jnp.transpose(stacked, (1, 0, 2)).reshape(stacked.shape[1], -1)
    batch_loss, pull_back = jax.vjp(partial(batch_objective, labels=labels), pooled_sum)
    sum_grad = pull_back(jnp.ones_like(batch_loss) * loss_scale)[0]

    def backward(running, block_index):
        logits, weight_block = block_logits(block_index)
        soft_plus = jax.nn.softplus(logits)
        saturated = jnp.log1p(soft_plus)
        offset = (block_index * block_size).astype(jnp.int32)
        grad_block = lax.dynamic_slice_in_dim(sum_grad, offset, block_size, 1)
        excess_grad = lax.dot_general(pool_weights, grad_block, (((0,), (0,)), ((), ())), precision=precise, preferred_element_type=jnp.float32)
        logit_grad = (excess_grad * pool_power * (1.0 + saturated) ** (pool_power - 1.0) * jax.nn.sigmoid(logits) / (1.0 + soft_plus)).astype(jnp.bfloat16)
        block_grad = lax.dot_general(hidden, logit_grad, (((0,), (0,)), ((), ())), preferred_element_type=jnp.float32).astype(jnp.bfloat16)
        running = running + lax.dot_general(logit_grad, weight_block, (((1,), (1,)), ((), ())), preferred_element_type=jnp.float32)
        return (running, block_grad)
    start_grad = jnp.zeros((hidden.shape[0], hidden.shape[1]), jnp.float32)
    hidden_grad, block_grads = lax.scan(backward, start_grad, indices)
    weight_grad = jnp.transpose(block_grads, (1, 0, 2)).reshape(hidden.shape[1], -1)
    return (batch_loss, weight_grad, hidden_grad)
```

```python
import functools

import jax
import jax.numpy as jnp
from jax import lax
from jax.experimental import pallas as pl
from jax.experimental.pallas import tpu as pltpu
from jax.sharding import PartitionSpec as P

MESH = pl.DeviceIdType.MESH
F32, BF16 = jnp.float32, jnp.bfloat16

SEQ_GROUP = 4
GROUPS = 16
TOK = 32
SIDE = 4
DEPTH = 8
TAG = 128

score_scale = 20.0
loss_scale = 65536.0
norm_eps = 1e-06
precise = lax.Precision.HIGHEST

GATHER_COPIES = 24
PAIR = 16


def iota(shape, dim):
    return lax.broadcasted_iota(jnp.int32, shape, dim)


def split3(x):
    first = x.astype(BF16)
    rest = x - first.astype(F32)
    second = rest.astype(BF16)
    third = (rest - second.astype(F32)).astype(BF16)
    return first, second, third


def dot(a, b, dims=((1,), (0,)), precision=None):
    return lax.dot_general(a, b, (dims, ((), ())), precision=precision, preferred_element_type=F32)


def fused(
    hidden_ref, weight_ref, bias_ref, seq_ref, mask_ref, labels_ref,
    loss_ref, wgrad_ref, hgrad_ref,
    hid, w, wsib, logit, fac, excess, mt, lg, lgp, lgs,
    ara, arb, part, farl, farr, fromm, fromp, acc, rtwo, zsend, zrecv, wg,
    loc_sem, g_send, g_recv, e_send, e_recv, a_send, a_recv, b_send, b_recv,
    r_send, r_recv, s_send, s_recv, z_send, z_recv,
):
    width = hidden_ref.shape[1]
    half = width // 2
    voc = weight_ref.shape[1]
    d, v = lax.axis_index("dp"), lax.axis_index("vocab")
    core, y, xh = d % 2, (d // 2) % 4, d // 8
    xl, z = v % 2, v // 2
    x = xh * 2 + xl

    def place(px, py, pc, pz):
        return ((px // 2) * 8 + py * 2 + pc, pz * 2 + px % 2)

    def group(gxh, gy, gc):
        return gxh * 8 + gy * 2 + gc

    def column_mate(k):
        return place(x, y, (core + k // DEPTH) % 2, (z + k % DEPTH) % DEPTH)

    def plane_mate(k):
        return place((x + k // SIDE) % SIDE, (y + k % SIDE) % SIDE, core, z)

    def remote(src, dst, send, recv, device):
        return pltpu.make_async_remote_copy(
            src_ref=src, dst_ref=dst, send_sem=send, recv_sem=recv, device_id=device, device_id_type=MESH
        )

    w_copies = [
        pltpu.make_async_copy(weight_ref.at[pl.ds(h * half, half), :], w.at[h], loc_sem.at[h]) for h in range(2)
    ]
    h_copies = [
        pltpu.make_async_copy(
            hidden_ref.at[:, pl.ds(h * half, half)], hid.at[d, h, :, pl.ds(0, half)], loc_sem.at[2 + h]
        )
        for h in range(2)
    ]
    for copy in h_copies + w_copies:
        copy.start()

    barrier = pltpu.get_barrier_semaphore()
    for k in range(1, PAIR):
        pl.semaphore_signal(barrier, inc=1, device_id=column_mate(k), device_id_type=MESH)
        pl.semaphore_signal(barrier, inc=1, device_id=plane_mate(k), device_id_type=MESH)

    tag_row = jnp.where(mask_ref[...] > 0, seq_ref[...], SEQ_GROUP).astype(F32)
    eye = iota((TOK, TOK), 0) == iota((TOK, TOK), 1)
    tag_col = jnp.sum(jnp.where(eye, jnp.broadcast_to(tag_row, (TOK, TOK)), 0.0), axis=1, keepdims=True)
    tag_block = jnp.broadcast_to(tag_col, (TOK, TAG)).astype(BF16)
    for h in range(2):
        hid[d, h, :, pl.ds(half, TAG)] = tag_block
    for copy in h_copies:
        copy.wait()
    pl.semaphore_wait(barrier, 2 * (PAIR - 1))

    up, down = (y + 1) % 4, (y + 3) % 4
    far = (y + 2) % 4
    to_up, to_down = place(x, up, core, z), place(x, down, core, z)
    other = 1 - xh
    to_cross = place(other * 2 + 1 - xl, y, core, z)
    to_twin = place(xh * 2 + 1 - xl, y, core, z)
    to_sib = place(x, y, 1 - core, z)
    sent = []

    def gsend(k, chunk, device):
        copy = remote(chunk, chunk, g_send.at[k], g_recv.at[k], device)
        copy.start()
        sent.append(copy)

    def gwait(k, chunk):
        remote(chunk, chunk, g_send.at[k], g_recv.at[k], to_sib).wait_recv()

    own = hid.at[d]
    c_down, c_up, c_far = (hid.at[group(xh, yy, core)] for yy in (down, up, far))
    cross_y = (y, down, up, far)

    gsend(0, own, to_up)
    gsend(1, own, to_down)
    gsend(2, hid.at[d, 1 - xl], to_cross)
    gsend(3, own, to_sib)

    def crossed(i, k):
        chunk = hid.at[group(other, cross_y[i], core), xl]
        gwait(k, chunk)
        gsend(12 + i, chunk, to_twin)
        gsend(16 + i, chunk, to_sib)

    crossed(0, 2)
    gwait(0, c_down)
    gsend(4, hid.at[group(xh, down, core), 0], to_up)
    gsend(5, hid.at[group(xh, down, core), 1 - xl], to_cross)
    gsend(6, c_down, to_sib)
    gwait(1, c_up)
    gsend(7, hid.at[group(xh, up, core), 1], to_down)
    gsend(8, hid.at[group(xh, up, core), 1 - xl], to_cross)
    gsend(9, c_up, to_sib)
    gwait(4, hid.at[group(xh, far, core), 0])
    gwait(7, hid.at[group(xh, far, core), 1])
    gsend(10, hid.at[group(xh, far, core), 1 - xl], to_cross)
    gsend(11, c_far, to_sib)
    crossed(1, 5)
    crossed(2, 8)
    crossed(3, 10)
    for i in range(4):
        chunk = hid.at[group(other, cross_y[i], core), 1 - xl]
        gwait(12 + i, chunk)
        gsend(20 + i, chunk, to_sib)

    for copy in w_copies:
        copy.wait()
    w_swap = remote(w.at[1 - core], wsib, e_send.at[0], e_recv.at[0], to_sib)
    w_swap.start()

    gwait(3, hid.at[group(xh, y, 1 - core)])
    gwait(6, hid.at[group(xh, down, 1 - core)])
    gwait(9, hid.at[group(xh, up, 1 - core)])
    gwait(11, hid.at[group(xh, far, 1 - core)])
    for i in range(4):
        gwait(16 + i, hid.at[group(other, cross_y[i], 1 - core), xl])
        gwait(20 + i, hid.at[group(other, cross_y[i], 1 - core), 1 - xl])

    tokens = GROUPS * TOK
    deep = min(512, half)
    per_half = half // deep

    logit[...] = jnp.broadcast_to(bias_ref[...], (tokens, voc))

    def logit_step(i, carry):
        h = i // per_half
        start = pl.multiple_of((i % per_half) * deep, deep)
        a = hid[:, h, :, pl.ds(start, deep)].reshape(tokens, deep)
        logit[...] += dot(a, w[h, pl.ds(start, deep), :])
        return carry

    lax.fori_loop(0, 2 * per_half, logit_step, 0)

    tags = hid[:, 0, :, pl.ds(half, TAG)].reshape(tokens, TAG).astype(F32)
    lane = iota((tokens, TAG), 1)
    index = lane % 32
    wanted_group = index // 2
    wanted_tag = index % 2 + 2 * (lane // 32)
    belongs = (
        (iota((tokens, TAG), 0) // TOK == wanted_group)
        & (tags == wanted_tag.astype(F32))
        & (tags < SEQ_GROUP)
        & (lane < 64)
    )
    member_t = jnp.where(belongs, 1.0, 0.0)
    mt[...] = member_t.astype(BF16)
    member = jnp.transpose(member_t)
    inv_count = 1.0 / jnp.maximum(jnp.sum(member, axis=1, keepdims=True), 1.0)
    member = member.astype(BF16)

    def excess_step(i, carry):
        rows = pl.ds(pl.multiple_of(i * TOK, TOK), TOK)
        l = logit[rows, :]
        soft = jnp.maximum(l, 0.0) + jnp.log1p(jnp.exp(-jnp.abs(l)))
        u = 1.0 + jnp.log1p(soft)
        u2 = u * u
        excess[rows, :] = u2 * u2 - 1.0
        return carry

    lax.fori_loop(0, GROUPS, excess_step, 0)
    e1, e2, e3 = split3(excess[...])
    pooled_sum = (dot(member, e1) + dot(member, e2) + dot(member, e3)) * inv_count
    pooled = jnp.log1p(pooled_sum) * 0.25

    wide = iota((32, TAG), 1)
    in_passages = (wide >= 32) & (wide < 64)
    inner = dot(pooled[:32], pooled, ((1,), (1,)), precise)
    inner = jnp.where(in_passages, inner, 0.0)
    packed = inner[0:8]
    packed = pltpu.roll(packed, 96, 1)
    for b in range(1, 4):
        shift = 32 * (b - 1)
        piece = inner[8 * b : 8 * b + 8]
        packed = packed + (pltpu.roll(piece, shift, 1) if shift else piece)
    squares = dot(jnp.ones((8, voc), F32), pooled * pooled, ((1,), (1,)), precise)

    slot = core * DEPTH + z
    ara[slot, 0:8, :] = packed
    ara[slot, 8:16, :] = squares
    a_copies = [
        remote(ara.at[slot], ara.at[slot], a_send.at[k], a_recv.at[k], column_mate(k)) for k in range(1, PAIR)
    ]
    for copy in a_copies:
        copy.start()

    def factor_step(i, carry):
        rows = pl.ds(pl.multiple_of(i * TOK, TOK), TOK)
        l = logit[rows, :]
        e = jnp.exp(-jnp.abs(l))
        soft = jnp.maximum(l, 0.0) + jnp.log1p(e)
        u = 1.0 + jnp.log1p(soft)
        top = jnp.where(l >= 0.0, 1.0, e)
        fac[rows, :] = 4.0 * (u * u * u) * top / ((1.0 + e) * (1.0 + soft))
        return carry

    lax.fori_loop(0, GROUPS, factor_step, 0)

    for copy in a_copies:
        copy.wait_recv()
    column_sum = ara[0]
    for k in range(1, PAIR):
        column_sum = column_sum + ara[k]
    slot_b = x * SIDE + y
    arb[slot_b] = column_sum
    b_copies = [
        remote(arb.at[slot_b], arb.at[slot_b], b_send.at[k], b_recv.at[k], plane_mate(k)) for k in range(1, PAIR)
    ]
    for copy in b_copies:
        copy.start()
    for copy in b_copies:
        copy.wait_recv()
    total = arb[0]
    for k in range(1, PAIR):
        total = total + arb[k]

    pieces = []
    for b in range(4):
        shift = (32 - 32 * b) % 128
        pieces.append(pltpu.roll(total[0:8], shift, 1) if shift else total[0:8])
    inner = jnp.where(in_passages, jnp.concatenate(pieces, axis=0), 0.0)
    square_row = total[8:9]
    eye_wide = iota((TAG, TAG), 0) == iota((TAG, TAG), 1)
    square_col = jnp.sum(jnp.where(eye_wide, jnp.broadcast_to(square_row, (TAG, TAG)), 0.0), axis=1, keepdims=True)
    norm_row = jnp.sqrt(square_row + norm_eps)
    norm_col = jnp.sqrt(square_col + norm_eps)
    cosine = inner / (norm_col[:32] * norm_row)
    scores = score_scale * cosine
    exp_scores = jnp.where(in_passages, jnp.exp(scores), 0.0)
    totals = jnp.sum(exp_scores, axis=0, keepdims=True)
    totals = jnp.where(in_passages[0:1], totals, 1.0)
    labels = labels_ref[...].astype(F32)
    label_col = jnp.sum(jnp.where(eye, jnp.broadcast_to(labels, (32, 32)), 0.0), axis=1, keepdims=True)
    row_id = iota((32, TAG), 0)
    label_row = jnp.sum(
        jnp.where(wide - 32 == row_id, jnp.broadcast_to(label_col, (32, TAG)), 0.0), axis=0, keepdims=True
    )
    chosen = jnp.where((row_id.astype(F32) == label_row) & in_passages, 1.0, 0.0)
    per_passage = jnp.log(totals) - jnp.sum(chosen * scores, axis=0, keepdims=True)
    loss_ref[...] = jnp.sum(per_passage, axis=1, keepdims=True) / 32.0
    score_grad = (loss_scale * score_scale / 32.0) * (exp_scores / totals - chosen)
    blank = jnp.zeros((TAG - 32, TAG), F32)
    grad_full = jnp.concatenate([score_grad, blank], axis=0)
    cos_full = jnp.concatenate([cosine, blank], axis=0)
    grad_sym = grad_full + jnp.transpose(grad_full)
    cos_sym = cos_full + jnp.transpose(cos_full)
    radial = jnp.sum(grad_sym * cos_sym, axis=1, keepdims=True)
    inv_norm = 1.0 / norm_col
    unit = pooled * inv_norm
    pooled_grad = (dot(grad_sym, unit, precision=precise) - unit * radial) * inv_norm
    sum_grad = pooled_grad * inv_count / (4.0 * (1.0 + pooled_sum))

    s1, s2, s3 = split3(sum_grad)
    new, old = iota((64, 64), 0), iota((64, 64), 1)
    source = ((new // 16) % 2) * 32 + ((new // 2) % 8) * 4 + (new // 32) * 2 + new % 2
    shuffle = jnp.where(source == old, 1.0, 0.0).astype(BF16)

    def grad_step(i, carry):
        rows = pl.ds(pl.multiple_of(i * 64, 64), 64)
        m = mt[rows, :]
        g = (dot(m, s1) + dot(m, s2) + dot(m, s3)) * fac[rows, :]
        g = g.astype(BF16)
        lg[rows, :] = g
        p = dot(shuffle, g).astype(BF16)
        lgp[(i // 4) * 2, i % 4] = p[:32]
        lgp[(i // 4) * 2 + 1, i % 4] = p[32:]
        return carry

    lax.fori_loop(0, 8, grad_step, 0)
    lg_swap = remote(lgp, lgs, e_send.at[1], e_recv.at[1], to_sib)
    lg_swap.start()
    w_swap.wait_recv()
    lg_swap.wait_recv()

    block = min(512, half)

    def partial(o):
        def rows_of(ref):
            picked = []
            for i in range(4):
                px = (1 - core) * ((x + o) % 4) + core * i
                py = core * ((y + o) % 4) + (1 - core) * i
                picked.append(ref[px, py])
            return jnp.concatenate(picked, axis=0)

        mine, theirs = rows_of(lgp), rows_of(lgs)

        def step(n, carry):
            start = pl.multiple_of(n * block, block)
            cols = pl.ds(start, block)
            value = dot(mine, w[core, cols, :], ((1,), (1,))) + dot(theirs, wsib[cols, :], ((1,), (1,)))
            part[o, :, :, cols] = value.astype(BF16).reshape(4, 32, block)
            return carry

        lax.fori_loop(0, half // block, step, 0)

    quarter = half // 2
    left, right = pl.ds(0, quarter), pl.ds(quarter, quarter)

    def ring(o):
        return place((x + (1 - core) * o) % 4, (y + core * o) % 4, core, z)

    def ring_two(o):
        return place((x + core * o) % 4, (y + (1 - core) * o) % 4, core, z)

    plus, minus = ring(1), ring(3)
    partial(2)
    far_l = remote(part.at[2, :, :, left], farl, r_send.at[0], r_recv.at[0], plus)
    far_r = remote(part.at[2, :, :, right], farr, r_send.at[1], r_recv.at[1], minus)
    far_l.start()
    far_r.start()
    partial(1)
    plain_r = remote(part.at[1, :, :, right], fromm.at[1], r_send.at[2], r_recv.at[2], plus)
    plain_r.start()
    partial(3)
    plain_l = remote(part.at[3, :, :, left], fromp.at[0], r_send.at[3], r_recv.at[3], minus)
    plain_l.start()
    partial(0)
    far_l.wait_recv()
    part[1, :, :, left] = (part[1, :, :, left].astype(F32) + farl[...].astype(F32)).astype(BF16)
    sum_l = remote(part.at[1, :, :, left], fromm.at[0], r_send.at[4], r_recv.at[4], plus)
    sum_l.start()
    far_r.wait_recv()
    part[3, :, :, right] = (part[3, :, :, right].astype(F32) + farr[...].astype(F32)).astype(BF16)
    sum_r = remote(part.at[3, :, :, right], fromp.at[1], r_send.at[5], r_recv.at[5], minus)
    sum_r.start()

    def weight_step(i, carry):
        h = i // per_half
        start = pl.multiple_of((i % per_half) * deep, deep)
        a = hid[:, h, :, pl.ds(start, deep)].reshape(tokens, deep)
        wg[h, pl.ds(start, deep), :] = dot(a, lg[...], ((0,), (0,))).astype(BF16)
        return carry

    lax.fori_loop(0, 2 * per_half, weight_step, 0)
    wg_copies = [
        pltpu.make_async_copy(wg.at[h], wgrad_ref.at[pl.ds(h * half, half), :], loc_sem.at[4 + h]) for h in range(2)
    ]
    for copy in wg_copies:
        copy.start()

    for copy in (plain_r, plain_l, sum_l, sum_r):
        copy.wait_recv()
    for h, cols in ((0, left), (1, right)):
        value = part[0, :, :, cols].astype(F32) + fromm[h].astype(F32) + fromp[h].astype(F32)
        acc[:, :, cols] = value.astype(BF16)

    seat = core * x + (1 - core) * y
    two_copies = [
        remote(acc.at[(seat + o) % 4], rtwo.at[o - 1], s_send.at[o - 1], s_recv.at[o - 1], ring_two(o))
        for o in range(1, 4)
    ]
    for copy in two_copies:
        copy.start()
    for copy in two_copies:
        copy.wait_recv()
    rows = acc[seat].astype(F32)
    for o in range(3):
        rows = rows + rtwo[o].astype(F32)
    rows = rows.astype(BF16)

    slab = half // 8
    stacked = jnp.concatenate([rows[:, b * slab : (b + 1) * slab] for b in range(8)], axis=0)
    new, old = iota((256, 256), 0), iota((256, 256), 1)
    source = (new % 8) * 32 + (new // 16) * 2 + (new // 8) % 2
    shuffle = jnp.where(source == old, 1.0, 0.0).astype(BF16)
    zsend[...] = dot(shuffle, stacked).astype(BF16).reshape(16, 16, slab)
    z_copies = []
    for k in range(1, PAIR):
        target = ((core + k // DEPTH) % 2) * DEPTH + (z + k % DEPTH) % DEPTH
        copy = remote(zsend.at[target], zrecv.at[slot], z_send.at[k], z_recv.at[k], column_mate(k))
        copy.start()
        z_copies.append(copy)
    zrecv[slot] = zsend[slot]
    for copy in z_copies:
        copy.wait_recv()
    for c in range(2):
        value = zrecv[c * DEPTH].astype(F32)
        for k in range(1, DEPTH):
            value = value + zrecv[c * DEPTH + k].astype(F32)
        for r in range(2):
            for b in range(8):
                hgrad_ref[r : r + 1, pl.ds(c * half + b * slab, slab)] = value[r * 8 + b : r * 8 + b + 1]

    for copy in sent + [w_swap, lg_swap] + a_copies + b_copies:
        copy.wait_send()
    for copy in [far_l, far_r, plain_r, plain_l, sum_l, sum_r] + two_copies + z_copies:
        copy.wait_send()
    for copy in wg_copies:
        copy.wait()


def body(hidden, head_weight, vocab_bias, seq_ids, token_mask, labels):
    width, voc = head_weight.shape
    half = width // 2
    tokens = GROUPS * TOK
    vmem = pl.BlockSpec(memory_space=pltpu.VMEM)
    hbm = pl.BlockSpec(memory_space=pl.ANY)
    dma = pltpu.SemaphoreType.DMA
    loss, weight_grad, hidden_grad = pl.pallas_call(
        fused,
        out_shape=(
            jax.ShapeDtypeStruct((1, 1), F32),
            jax.ShapeDtypeStruct((width, voc), BF16),
            jax.ShapeDtypeStruct((2, width), F32),
        ),
        in_specs=[hbm, hbm, vmem, vmem, vmem, vmem],
        out_specs=(vmem, hbm, vmem),
        scratch_shapes=[
            pltpu.VMEM((GROUPS, 2, TOK, half + TAG), BF16),
            pltpu.VMEM((2, half, voc), BF16),
            pltpu.VMEM((half, voc), BF16),
            pltpu.VMEM((tokens, voc), F32),
            pltpu.VMEM((tokens, voc), F32),
            pltpu.VMEM((tokens, voc), F32),
            pltpu.VMEM((tokens, TAG), BF16),
            pltpu.VMEM((tokens, voc), BF16),
            pltpu.VMEM((4, 4, TOK, voc), BF16),
            pltpu.VMEM((4, 4, TOK, voc), BF16),
            pltpu.VMEM((PAIR, 16, TAG), F32),
            pltpu.VMEM((PAIR, 16, TAG), F32),
            pltpu.VMEM((4, 4, TOK, half), BF16),
            pltpu.VMEM((4, TOK, half // 2), BF16),
            pltpu.VMEM((4, TOK, half // 2), BF16),
            pltpu.VMEM((2, 4, TOK, half // 2), BF16),
            pltpu.VMEM((2, 4, TOK, half // 2), BF16),
            pltpu.VMEM((4, TOK, half), BF16),
            pltpu.VMEM((3, TOK, half), BF16),
            pltpu.VMEM((PAIR, 16, half // 8), BF16),
            pltpu.VMEM((PAIR, 16, half // 8), BF16),
            pltpu.VMEM((2, half, voc), BF16),
            dma((6,)),
            dma((GATHER_COPIES,)),
            dma((GATHER_COPIES,)),
            dma((2,)),
            dma((2,)),
            dma((PAIR,)),
            dma((PAIR,)),
            dma((PAIR,)),
            dma((PAIR,)),
            dma((6,)),
            dma((6,)),
            dma((3,)),
            dma((3,)),
            dma((PAIR,)),
            dma((PAIR,)),
        ],
        compiler_params=pltpu.CompilerParams(
            collective_id=0, has_side_effects=True, vmem_limit_bytes=48 * 1024 * 1024
        ),
        name="splade_head",
    )(
        hidden,
        head_weight,
        vocab_bias.reshape(1, voc),
        seq_ids,
        token_mask,
        labels.reshape(1, labels.shape[0]),
    )
    return loss.reshape(()), weight_grad, hidden_grad


def solution(mesh):
    in_specs = (
        P("dp", None),
        P(None, ("dp", "vocab")),
        P(("dp", "vocab")),
        P("dp", None),
        P("dp", None),
        P(),
    )
    out_specs = (P(), P(None, ("dp", "vocab")), P(("dp", "vocab"), None))
    return jax.shard_map(body, mesh=mesh, in_specs=in_specs, out_specs=out_specs, check_vma=False)
```

```python
import functools

import jax
import jax.numpy as jnp
from jax import lax
from jax.experimental import pallas as pl
from jax.experimental.pallas import tpu as pltpu
from jax.sharding import PartitionSpec as P

MESH = pl.DeviceIdType.MESH
F32, BF16 = jnp.float32, jnp.bfloat16

SEQ_GROUP = 4
GROUPS = 16
TOK = 32
SIDE = 4
DEPTH = 8
TAG = 128

score_scale = 20.0
loss_scale = 65536.0
norm_eps = 1e-06
precise = lax.Precision.HIGHEST

GATHER_COPIES = 28
PAIR = 16


def iota(shape, dim):
    return lax.broadcasted_iota(jnp.int32, shape, dim)


def split3(x):
    first = x.astype(BF16)
    rest = x - first.astype(F32)
    second = rest.astype(BF16)
    third = (rest - second.astype(F32)).astype(BF16)
    return first, second, third


def dot(a, b, dims=((1,), (0,)), precision=None):
    return lax.dot_general(a, b, (dims, ((), ())), precision=precision, preferred_element_type=F32)


def fused(
    hidden_ref, weight_ref, rows_ref,
    loss_ref, wgrad_ref, hgrad_ref,
    hid, tags_ref, w, wsib, logit, fac, excess, mt, lg, lgp, lgs,
    ara, arb, pre, part, farl, farr, fromm, fromp, acc, rtwo, zsend, zrecv,
    loc_sem, g_send, g_recv, h_send, h_recv, t_send, t_recv, e_send, e_recv, a_send, a_recv, b_send, b_recv,
    r_send, r_recv, s_send, s_recv, z_send, z_recv,
):
    width = hidden_ref.shape[1]
    half = width // 2
    voc = weight_ref.shape[1]
    d, v = lax.axis_index("dp"), lax.axis_index("vocab")
    core, y, xh = d % 2, (d // 2) % 4, d // 8
    xl, z = v % 2, v // 2
    x = xh * 2 + xl

    def place(px, py, pc, pz):
        return ((px // 2) * 8 + py * 2 + pc, pz * 2 + px % 2)

    def group(gxh, gy, gc):
        return gxh * 8 + gy * 2 + gc

    def column_mate(k):
        return place(x, y, (core + k // DEPTH) % 2, (z + k % DEPTH) % DEPTH)

    def plane_mate(k):
        return place((x + k // SIDE) % SIDE, (y + k % SIDE) % SIDE, core, z)

    def remote(src, dst, send, recv, device):
        return pltpu.make_async_remote_copy(
            src_ref=src, dst_ref=dst, send_sem=send, recv_sem=recv, device_id=device, device_id_type=MESH
        )

    sent = []

    def launch(copy):
        copy.start()
        sent.append(copy)

    w_copies = [
        pltpu.make_async_copy(weight_ref.at[pl.ds(h * half, half), :], w.at[h], loc_sem.at[h]) for h in range(2)
    ]
    quad = width // 4
    h_copies = [
        pltpu.make_async_copy(hidden_ref.at[:, pl.ds(q * quad, quad)], hid.at[d, q], loc_sem.at[2 + q]) for q in range(4)
    ]
    for copy in h_copies + w_copies:
        copy.start()

    barrier = pltpu.get_barrier_semaphore()
    for k in range(1, PAIR):
        pl.semaphore_signal(barrier, inc=1, device_id=column_mate(k), device_id_type=MESH)
        pl.semaphore_signal(barrier, inc=1, device_id=plane_mate(k), device_id_type=MESH)

    eye = iota((TOK, TOK), 0) == iota((TOK, TOK), 1)
    tag_row = rows_ref[2:3, 0:TOK]
    tag_col = jnp.sum(jnp.where(eye, jnp.broadcast_to(tag_row, (TOK, TOK)), 0.0), axis=1, keepdims=True)
    seat_t = xh * 4 + y
    tags_ref[core, seat_t] = jnp.broadcast_to(tag_col, (TOK, TAG)).astype(BF16)
    pl.semaphore_wait(barrier, 2 * (PAIR - 1))

    up, down, far = (y + 1) % 4, (y + 3) % 4, (y + 2) % 4
    other = 1 - xh
    cross_x = other * 2 + 1 - xl
    colour = (z + 2 * xl) % 4
    to_sib = place(x, y, 1 - core, z)
    to_twin = place(xh * 2 + 1 - xl, y, core, z)
    to_above = place(x, y, core, (z + 1) % DEPTH)
    to_below = place(x, y, core, (z + DEPTH - 1) % DEPTH)

    def spot(n, rq, of_core=core):
        row = group(xh if n < 4 else other, (y, up, down, far)[n % 4], of_core)
        return hid.at[row, (colour + rq) % 4]

    fetches = (
        (place(cross_x, y, core, z), 4, 2, (0, 1, 3)),
        (place(x, down, core, z), 1, 0, (0, 2, 1)),
        (place(x, up, core, z), 2, 0, (0, 2, 3)),
        (place(x, far, core, z), 3, 0, (0,)),
        (place(cross_x, down, core, z), 5, 2, (0,)),
        (place(cross_x, up, core, z), 6, 2, (0,)),
        (place(cross_x, far, core, z), 7, 2, (0,)),
    )
    count = 0
    for level in range(3):
        for device, n, shift, quarters in fetches:
            if level < len(quarters):
                rq = quarters[level]
                q = (colour + shift + rq) % 4
                src = hidden_ref.at[:, pl.ds(pl.multiple_of(q * quad, quad), quad)]
                launch(remote(src, hid.at[d, q], g_send.at[count], g_recv.at[n * 4 + rq], device))
                count += 1
    own_tags = tags_ref.at[core, seat_t]
    for device, n, _, _ in fetches:
        launch(remote(own_tags, own_tags, t_send.at[n], t_recv.at[n], device))
    for copy in h_copies:
        copy.wait()

    def hand_over(n, rq):
        chunk = spot(n, rq)
        launch(remote(chunk, chunk, h_send.at[n * 4 + rq], h_recv.at[n * 4 + rq], to_sib))

    def arrived(n, rq):
        chunk = spot(n, rq)
        remote(chunk, chunk, g_send.at[0], g_recv.at[n * 4 + rq], to_sib).wait_recv()

    for rq in range(4):
        hand_over(0, rq)
    for copy in w_copies:
        copy.wait()
    w_swap = remote(w.at[1 - core], wsib, e_send.at[0], e_recv.at[0], to_sib)
    launch(w_swap)

    for n in (4, 1, 2, 3, 5, 6, 7):
        arrived(n, 0)
        chunk = spot(n, 0)
        for device, rq, skipped in ((to_twin, 2, (1, 2)), (to_above, 3, (2, 4)), (to_below, 1, (1, 4))):
            if n not in skipped:
                launch(remote(chunk, chunk, g_send.at[count], g_recv.at[n * 4 + rq], device))
                count += 1
        hand_over(n, 0)
    for n in range(1, 8):
        there = tags_ref.at[core, (xh if n < 4 else other) * 4 + (y, up, down, far)[n % 4]]
        remote(there, there, t_send.at[n], t_recv.at[n], to_sib).wait_recv()
    launch(remote(tags_ref.at[core], tags_ref.at[core], t_send.at[0], t_recv.at[0], to_sib))
    for n in (4, 1, 2, 3, 5, 6, 7):
        for rq in (2, 3, 1):
            arrived(n, rq)
            hand_over(n, rq)

    remote(tags_ref.at[1 - core], tags_ref.at[1 - core], t_send.at[0], t_recv.at[0], to_sib).wait_recv()
    for n in range(8):
        for rq in range(4):
            chunk = spot(n, rq, 1 - core)
            remote(chunk, chunk, h_send.at[0], h_recv.at[n * 4 + rq], to_sib).wait_recv()

    tokens = GROUPS * TOK
    deep = min(512, quad)
    per_half = half // deep
    per_quad = quad // deep

    logit[...] = jnp.broadcast_to(rows_ref[0:1, :], (tokens, voc))

    def logit_step(i, carry):
        start = pl.multiple_of((i % per_quad) * deep, deep)
        a = hid[:, i // per_quad, :, pl.ds(start, deep)].reshape(tokens, deep)
        rows = pl.ds(pl.multiple_of((i % per_half) * deep, deep), deep)
        logit[...] += dot(a, w[i // per_half, rows, :])
        return carry

    lax.fori_loop(0, 2 * per_half, logit_step, 0)

    by_group = [tags_ref[c, gxh * 4 + gy] for gxh in range(2) for gy in range(4) for c in range(2)]
    tags = jnp.concatenate(by_group, axis=0).astype(F32)
    lane = iota((tokens, TAG), 1)
    index = lane % 32
    wanted_group = index // 2
    wanted_tag = index % 2 + 2 * (lane // 32)
    belongs = (
        (iota((tokens, TAG), 0) // TOK == wanted_group)
        & (tags == wanted_tag.astype(F32))
        & (tags < SEQ_GROUP)
        & (lane < 64)
    )
    member_t = jnp.where(belongs, 1.0, 0.0)
    for i in range(3):
        mt[:, pl.ds(i * TAG, TAG)] = member_t.astype(BF16)
    member = jnp.transpose(member_t)
    inv_count = 1.0 / jnp.maximum(jnp.sum(member, axis=1, keepdims=True), 1.0)
    member = member.astype(BF16)

    def excess_step(i, carry):
        rows = pl.ds(pl.multiple_of(i * TOK, TOK), TOK)
        l = logit[rows, :]
        soft = jnp.maximum(l, 0.0) + jnp.log1p(jnp.exp(-jnp.abs(l)))
        u = 1.0 + jnp.log1p(soft)
        u2 = u * u
        excess[rows, :] = u2 * u2 - 1.0
        return carry

    lax.fori_loop(0, GROUPS, excess_step, 0)
    e1, e2, e3 = split3(excess[...])
    pooled_sum = (dot(member, e1) + dot(member, e2) + dot(member, e3)) * inv_count
    pooled = jnp.log1p(pooled_sum) * 0.25

    wide = iota((32, TAG), 1)
    in_passages = (wide >= 32) & (wide < 64)
    inner = dot(pooled[:32], pooled, ((1,), (1,)), precise)
    inner = jnp.where(in_passages, inner, 0.0)
    packed = inner[0:8]
    packed = pltpu.roll(packed, 96, 1)
    for b in range(1, 4):
        shift = 32 * (b - 1)
        piece = inner[8 * b : 8 * b + 8]
        packed = packed + (pltpu.roll(piece, shift, 1) if shift else piece)
    squares = dot(jnp.ones((8, voc), F32), pooled * pooled, ((1,), (1,)), precise)

    slot = core * DEPTH + z
    ara[slot, 0:8, :] = packed
    ara[slot, 8:16, :] = squares
    a_copies = [
        remote(ara.at[slot], ara.at[slot], a_send.at[k], a_recv.at[k], column_mate(k)) for k in range(1, PAIR)
    ]
    for copy in a_copies:
        launch(copy)

    def factor_step(i, carry):
        rows = pl.ds(pl.multiple_of(i * TOK, TOK), TOK)
        l = logit[rows, :]
        e = jnp.exp(-jnp.abs(l))
        soft = jnp.maximum(l, 0.0) + jnp.log1p(e)
        u = 1.0 + jnp.log1p(soft)
        top = jnp.where(l >= 0.0, 1.0, e)
        fac[rows, :] = 4.0 * (u * u * u) * top / ((1.0 + e) * (1.0 + soft))
        return carry

    lax.fori_loop(0, GROUPS, factor_step, 0)

    for copy in a_copies:
        copy.wait_recv()
    column_sum = ara[0]
    for k in range(1, PAIR):
        column_sum = column_sum + ara[k]
    slot_b = x * SIDE + y
    arb[slot_b] = column_sum
    b_copies = [
        remote(arb.at[slot_b], arb.at[slot_b], b_send.at[k], b_recv.at[k], plane_mate(k)) for k in range(1, PAIR)
    ]
    for copy in b_copies:
        launch(copy)
    for copy in b_copies:
        copy.wait_recv()
    total = arb[0]
    for k in range(1, PAIR):
        total = total + arb[k]

    pieces = []
    for b in range(4):
        shift = (32 - 32 * b) % 128
        pieces.append(pltpu.roll(total[0:8], shift, 1) if shift else total[0:8])
    inner = jnp.where(in_passages, jnp.concatenate(pieces, axis=0), 0.0)
    square_row = total[8:9]
    eye_wide = iota((TAG, TAG), 0) == iota((TAG, TAG), 1)
    square_col = jnp.sum(jnp.where(eye_wide, jnp.broadcast_to(square_row, (TAG, TAG)), 0.0), axis=1, keepdims=True)
    norm_row = jnp.sqrt(square_row + norm_eps)
    norm_col = jnp.sqrt(square_col + norm_eps)
    cosine = inner / (norm_col[:32] * norm_row)
    scores = score_scale * cosine
    exp_scores = jnp.where(in_passages, jnp.exp(scores), 0.0)
    totals = jnp.sum(exp_scores, axis=0, keepdims=True)
    totals = jnp.where(in_passages[0:1], totals, 1.0)
    labels = rows_ref[1:2, 0:32]
    label_col = jnp.sum(jnp.where(eye, jnp.broadcast_to(labels, (32, 32)), 0.0), axis=1, keepdims=True)
    row_id = iota((32, TAG), 0)
    label_row = jnp.sum(
        jnp.where(wide - 32 == row_id, jnp.broadcast_to(label_col, (32, TAG)), 0.0), axis=0, keepdims=True
    )
    chosen = jnp.where((row_id.astype(F32) == label_row) & in_passages, 1.0, 0.0)
    per_passage = jnp.log(totals) - jnp.sum(chosen * scores, axis=0, keepdims=True)
    loss_ref[...] = jnp.sum(per_passage, axis=1, keepdims=True) / 32.0
    score_grad = (loss_scale * score_scale / 32.0) * (exp_scores / totals - chosen)
    blank = jnp.zeros((TAG - 32, TAG), F32)
    grad_full = jnp.concatenate([score_grad, blank], axis=0)
    cos_full = jnp.concatenate([cosine, blank], axis=0)
    grad_sym = grad_full + jnp.transpose(grad_full)
    cos_sym = cos_full + jnp.transpose(cos_full)
    radial = jnp.sum(grad_sym * cos_sym, axis=1, keepdims=True)
    inv_norm = 1.0 / norm_col
    unit = pooled * inv_norm
    pooled_grad = (dot(grad_sym, unit, precision=precise) - unit * radial) * inv_norm
    sum_grad = pooled_grad * inv_count / (4.0 * (1.0 + pooled_sum))

    thirds = jnp.concatenate(split3(sum_grad), axis=0)
    new, old = iota((128, 128), 0), iota((128, 128), 1)
    source = (new // 64) * 64 + ((new // 16) % 2) * 32 + ((new // 2) % 8) * 4 + ((new // 32) % 2) * 2 + new % 2
    shuffle = jnp.where(source == old, 1.0, 0.0).astype(BF16)
    lg_swaps = []
    for i in range(4):
        rows = pl.ds(i * 128, 128)
        g = (dot(mt[rows, :], thirds) * fac[rows, :]).astype(BF16)
        lg[rows, :] = g
        p = dot(shuffle, g).astype(BF16)
        box = (pl.ds((i // 2) * 2, 2), pl.ds((i % 2) * 2, 2))
        for b in range(4):
            lgp[(i // 2) * 2 + b % 2, (i % 2) * 2 + b // 2] = p[b * 32 : b * 32 + 32]
        swap = remote(lgp.at[box], lgs.at[box], e_send.at[1 + i], e_recv.at[1 + i], to_sib)
        launch(swap)
        lg_swaps.append(swap)

    block = min(512, half)

    def rows_of(ref, o):
        picked = []
        for i in range(4):
            px = (1 - core) * ((x + o) % 4) + core * i
            py = core * ((y + o) % 4) + (1 - core) * i
            picked.append(ref[px, py])
        return jnp.concatenate(picked, axis=0)

    def columns(n):
        return pl.ds(pl.multiple_of(n * block, block), block)

    def partial(o):
        mine, theirs = rows_of(lgp, o), rows_of(lgs, o)

        def step(n, carry):
            cols = columns(n)
            value = dot(mine, w[core, cols, :], ((1,), (1,))) + dot(theirs, wsib[cols, :], ((1,), (1,)))
            part[o, :, :, cols] = value.astype(BF16).reshape(4, 32, block)
            return carry

        lax.fori_loop(0, half // block, step, 0)

    mine = rows_of(lgp, 2)

    def first_step(n, carry):
        cols = columns(n)
        pre[:, cols] = dot(mine, w[core, cols, :], ((1,), (1,)))
        return carry

    lax.fori_loop(0, half // block, first_step, 0)
    w_swap.wait_recv()
    for swap in lg_swaps:
        swap.wait_recv()
    theirs = rows_of(lgs, 2)

    def second_step(n, carry):
        cols = columns(n)
        value = pre[:, cols] + dot(theirs, wsib[cols, :], ((1,), (1,)))
        part[2, :, :, cols] = value.astype(BF16).reshape(4, 32, block)
        return carry

    lax.fori_loop(0, half // block, second_step, 0)

    quarter = half // 2
    left, right = pl.ds(0, quarter), pl.ds(quarter, quarter)

    def ring(o):
        return place((x + (1 - core) * o) % 4, (y + core * o) % 4, core, z)

    def ring_two(o):
        return place((x + core * o) % 4, (y + (1 - core) * o) % 4, core, z)

    plus, minus = ring(1), ring(3)
    far_l = remote(part.at[2, :, :, left], farl, r_send.at[0], r_recv.at[0], plus)
    far_r = remote(part.at[2, :, :, right], farr, r_send.at[1], r_recv.at[1], minus)
    launch(far_l)
    launch(far_r)
    partial(1)
    plain_r = remote(part.at[1, :, :, right], fromm.at[1], r_send.at[2], r_recv.at[2], plus)
    launch(plain_r)
    partial(3)
    plain_l = remote(part.at[3, :, :, left], fromp.at[0], r_send.at[3], r_recv.at[3], minus)
    launch(plain_l)
    partial(0)
    far_l.wait_recv()
    part[1, :, :, left] = (part[1, :, :, left].astype(F32) + farl[...].astype(F32)).astype(BF16)
    sum_l = remote(part.at[1, :, :, left], fromm.at[0], r_send.at[4], r_recv.at[4], plus)
    launch(sum_l)
    far_r.wait_recv()
    part[3, :, :, right] = (part[3, :, :, right].astype(F32) + farr[...].astype(F32)).astype(BF16)
    sum_r = remote(part.at[3, :, :, right], fromp.at[1], r_send.at[5], r_recv.at[5], minus)
    launch(sum_r)

    def weight_step(i, carry):
        start = pl.multiple_of((i % per_quad) * deep, deep)
        a = hid[:, i // per_quad, :, pl.ds(start, deep)].reshape(tokens, deep)
        wgrad_ref[pl.ds(pl.multiple_of(i * deep, deep), deep), :] = dot(a, lg[...], ((0,), (0,))).astype(BF16)
        return carry

    lax.fori_loop(0, 2 * per_half, weight_step, 0)
    for copy in (plain_r, plain_l, sum_l, sum_r):
        copy.wait_recv()
    for h, cols in ((0, left), (1, right)):
        value = part[0, :, :, cols].astype(F32) + fromm[h].astype(F32) + fromp[h].astype(F32)
        acc[:, :, cols] = value.astype(BF16)

    seat = core * x + (1 - core) * y
    two_copies = [
        remote(acc.at[(seat + o) % 4], rtwo.at[o - 1], s_send.at[o - 1], s_recv.at[o - 1], ring_two(o))
        for o in range(1, 4)
    ]
    for copy in two_copies:
        launch(copy)
    for copy in two_copies:
        copy.wait_recv()
    rows = acc[seat].astype(F32)
    for o in range(3):
        rows = rows + rtwo[o].astype(F32)
    rows = rows.astype(BF16)

    slab = half // 8
    stacked = jnp.concatenate([rows[:, b * slab : (b + 1) * slab] for b in range(8)], axis=0)
    new, old = iota((256, 256), 0), iota((256, 256), 1)
    source = (new % 8) * 32 + (new // 16) * 2 + (new // 8) % 2
    shuffle = jnp.where(source == old, 1.0, 0.0).astype(BF16)
    zsend[...] = dot(shuffle, stacked).astype(BF16).reshape(16, 16, slab)
    z_copies = []
    for k in range(1, PAIR):
        target = ((core + k // DEPTH) % 2) * DEPTH + (z + k % DEPTH) % DEPTH
        copy = remote(zsend.at[target], zrecv.at[slot], z_send.at[k], z_recv.at[k], column_mate(k))
        launch(copy)
        z_copies.append(copy)
    zrecv[slot] = zsend[slot]
    for copy in z_copies:
        copy.wait_recv()
    for c in range(2):
        value = zrecv[c * DEPTH].astype(F32)
        for k in range(1, DEPTH):
            value = value + zrecv[c * DEPTH + k].astype(F32)
        for r in range(2):
            for b in range(8):
                hgrad_ref[r : r + 1, pl.ds(c * half + b * slab, slab)] = value[r * 8 + b : r * 8 + b + 1]

    for copy in sent:
        copy.wait_send()


def body(hidden, head_weight, vocab_bias, seq_ids, token_mask, labels):
    width, voc = head_weight.shape
    half = width // 2
    tokens = GROUPS * TOK
    tag = jnp.where(token_mask > 0, seq_ids, SEQ_GROUP).astype(F32)
    rows = jnp.concatenate(
        [
            vocab_bias[None, :],
            jnp.pad(labels.astype(F32)[None, :], ((0, 0), (0, voc - labels.shape[0]))),
            jnp.pad(tag, ((0, 5), (0, voc - TOK))),
        ],
        axis=0,
    )
    vmem = pl.BlockSpec(memory_space=pltpu.VMEM)
    hbm = pl.BlockSpec(memory_space=pltpu.HBM)
    dma = pltpu.SemaphoreType.DMA
    loss, weight_grad, hidden_grad = pl.pallas_call(
        fused,
        out_shape=(
            jax.ShapeDtypeStruct((1, 1), F32),
            jax.ShapeDtypeStruct((width, voc), BF16),
            jax.ShapeDtypeStruct((2, width), F32),
        ),
        in_specs=[hbm, hbm, vmem],
        out_specs=(vmem, vmem, vmem),
        scratch_shapes=[
            pltpu.VMEM((GROUPS, 4, TOK, width // 4), BF16),
            pltpu.VMEM((2, GROUPS // 2, TOK, TAG), BF16),
            pltpu.VMEM((2, half, voc), BF16),
            pltpu.VMEM((half, voc), BF16),
            pltpu.VMEM((tokens, voc), F32),
            pltpu.VMEM((tokens, voc), F32),
            pltpu.VMEM((tokens, voc), F32),
            pltpu.VMEM((tokens, 3 * TAG), BF16),
            pltpu.VMEM((tokens, voc), BF16),
            pltpu.VMEM((4, 4, TOK, voc), BF16),
            pltpu.VMEM((4, 4, TOK, voc), BF16),
            pltpu.VMEM((PAIR, 16, TAG), F32),
            pltpu.VMEM((PAIR, 16, TAG), F32),
            pltpu.VMEM((4 * TOK, half), F32),
            pltpu.VMEM((4, 4, TOK, half), BF16),
            pltpu.VMEM((4, TOK, half // 2), BF16),
            pltpu.VMEM((4, TOK, half // 2), BF16),
            pltpu.VMEM((2, 4, TOK, half // 2), BF16),
            pltpu.VMEM((2, 4, TOK, half // 2), BF16),
            pltpu.VMEM((4, TOK, half), BF16),
            pltpu.VMEM((3, TOK, half), BF16),
            pltpu.VMEM((PAIR, 16, half // 8), BF16),
            pltpu.VMEM((PAIR, 16, half // 8), BF16),
            dma((6,)),
            dma((GATHER_COPIES,)),
            dma((32,)),
            dma((32,)),
            dma((32,)),
            dma((8,)),
            dma((8,)),
            dma((5,)),
            dma((5,)),
            dma((PAIR,)),
            dma((PAIR,)),
            dma((PAIR,)),
            dma((PAIR,)),
            dma((6,)),
            dma((6,)),
            dma((3,)),
            dma((3,)),
            dma((PAIR,)),
            dma((PAIR,)),
        ],
        compiler_params=pltpu.CompilerParams(
            collective_id=0, has_side_effects=True, vmem_limit_bytes=48 * 1024 * 1024
        ),
        name="splade_head",
    )(hidden, head_weight, rows)
    return loss.reshape(()), weight_grad, hidden_grad


def solution(mesh):
    in_specs = (
        P("dp", None),
        P(None, ("dp", "vocab")),
        P(("dp", "vocab")),
        P("dp", None),
        P("dp", None),
        P(),
    )
    out_specs = (P(), P(None, ("dp", "vocab")), P(("dp", "vocab"), None))
    return jax.shard_map(body, mesh=mesh, in_specs=in_specs, out_specs=out_specs, check_vma=False)
```

```python
import functools

import jax
import jax.numpy as jnp
from jax import lax
from jax.experimental import pallas as pl
from jax.experimental.pallas import tpu as pltpu
from jax.sharding import PartitionSpec as P

MESH = pl.DeviceIdType.MESH
F32, BF16 = jnp.float32, jnp.bfloat16

SEQ_GROUP = 4
GROUPS = 16
TOK = 32
SIDE = 4
DEPTH = 8
TAG = 128

score_scale = 20.0
loss_scale = 65536.0
norm_eps = 1e-06
precise = lax.Precision.HIGHEST

GATHER_COPIES = 28
PAIR = 16
CHUNKS = 8


def iota(shape, dim):
    return lax.broadcasted_iota(jnp.int32, shape, dim)


def split3(x):
    first = x.astype(BF16)
    rest = x - first.astype(F32)
    second = rest.astype(BF16)
    third = (rest - second.astype(F32)).astype(BF16)
    return first, second, third


def dot(a, b, dims=((1,), (0,)), precision=None):
    return lax.dot_general(a, b, (dims, ((), ())), precision=precision, preferred_element_type=F32)


def fused(
    hidden_ref, weight_ref, bias_hbm, seq_hbm, mask_hbm, labels_hbm,
    loss_ref, wgrad_hbm, hgrad_ref,
    bias_ref, seq_ref, mask_ref, labels_ref, wgrad_ref,
    hid, tags_ref, w, wsib, logit, fac, excess, mt, lg, lgp, lgs,
    ara, arb, pre, part, fars_in, fromm, fromp, acc, rtwo, zsend, zrecv,
    loc_sem, g_send, g_recv, h_send, h_recv, t_send, t_recv, e_send, e_recv, a_send, a_recv, b_send, b_recv,
    r_send, r_recv, s_send, s_recv, z_send, z_recv,
):
    width = hidden_ref.shape[1]
    half = width // 2
    voc = weight_ref.shape[1]
    d, v = lax.axis_index("dp"), lax.axis_index("vocab")
    core, y, xh = d % 2, (d // 2) % 4, d // 8
    xl, z = v % 2, v // 2
    x = xh * 2 + xl

    def place(px, py, pc, pz):
        return ((px // 2) * 8 + py * 2 + pc, pz * 2 + px % 2)

    def column_mate(k):
        return place(x, y, (core + k // DEPTH) % 2, (z + k % DEPTH) % DEPTH)

    def plane_mate(k):
        return place((x + k // SIDE) % SIDE, (y + k % SIDE) % SIDE, core, z)

    def remote(src, dst, send, recv, device):
        return pltpu.make_async_remote_copy(
            src_ref=src, dst_ref=dst, send_sem=send, recv_sem=recv, device_id=device, device_id_type=MESH
        )

    sent = []

    def launch(copy):
        copy.start()
        sent.append(copy)

    w_copies = [
        pltpu.make_async_copy(weight_ref.at[pl.ds(h * half, half), :], w.at[h], loc_sem.at[h]) for h in range(2)
    ]
    quad = width // 4
    seat_t = xh * 4 + y
    h_copies = [
        pltpu.make_async_copy(hidden_ref.at[:, pl.ds(q * quad, quad)], hid.at[core, seat_t, q], loc_sem.at[2 + q])
        for q in range(4)
    ]
    small_copies = [
        pltpu.make_async_copy(src, dst, loc_sem.at[6 + i])
        for i, (src, dst) in enumerate(
            ((seq_hbm, seq_ref), (mask_hbm, mask_ref), (bias_hbm, bias_ref), (labels_hbm, labels_ref))
        )
    ]
    for copy in small_copies[:2] + h_copies + w_copies + small_copies[2:]:
        copy.start()

    barrier = pltpu.get_barrier_semaphore()
    for k in range(1, PAIR):
        pl.semaphore_signal(barrier, inc=1, device_id=column_mate(k), device_id_type=MESH)
        pl.semaphore_signal(barrier, inc=1, device_id=plane_mate(k), device_id_type=MESH)

    eye = iota((TOK, TOK), 0) == iota((TOK, TOK), 1)
    for copy in small_copies[:2]:
        copy.wait()
    tag_row = jnp.where(mask_ref[...] > 0, seq_ref[...], SEQ_GROUP).astype(F32)
    tag_col = jnp.sum(jnp.where(eye, jnp.broadcast_to(tag_row, (TOK, TOK)), 0.0), axis=1, keepdims=True)
    tags_ref[core, seat_t] = jnp.broadcast_to(tag_col, (TOK, TAG)).astype(BF16)
    pl.semaphore_wait(barrier, 2 * (PAIR - 1))

    up, down, far = (y + 1) % 4, (y + 3) % 4, (y + 2) % 4
    other = 1 - xh
    cross_x = other * 2 + 1 - xl
    colour = (z + 2 * xl) % 4
    to_sib = place(x, y, 1 - core, z)
    to_twin = place(xh * 2 + 1 - xl, y, core, z)
    to_above = place(x, y, core, (z + 1) % DEPTH)
    to_below = place(x, y, core, (z + DEPTH - 1) % DEPTH)

    def spot(n, rq, of_core=core):
        row = (xh if n < 4 else other) * 4 + (y, up, down, far)[n % 4]
        return hid.at[of_core, row, (colour + rq) % 4]

    fetches = (
        (place(cross_x, y, core, z), 4, 2, (0, 1, 3)),
        (place(x, down, core, z), 1, 0, (0, 2, 1)),
        (place(x, up, core, z), 2, 0, (0, 2, 3)),
        (place(x, far, core, z), 3, 0, (0,)),
        (place(cross_x, down, core, z), 5, 2, (0,)),
        (place(cross_x, up, core, z), 6, 2, (0,)),
        (place(cross_x, far, core, z), 7, 2, (0,)),
    )
    free_sends = iter(range(GATHER_COPIES))

    def post(chunks, levels):
        for level in levels:
            for device, n, shift, quarters in fetches:
                if n in chunks and level < len(quarters):
                    rq = quarters[level]
                    q = (colour + shift + rq) % 4
                    src = hid.at[core, seat_t, q]
                    launch(remote(src, src, g_send.at[next(free_sends)], g_recv.at[n * 4 + rq], device))

    for copy in h_copies:
        copy.wait()
    post((1, 2, 3, 4, 5, 6, 7), (0,))
    own_tags = tags_ref.at[core, seat_t]
    for device, n, _, _ in fetches:
        launch(remote(own_tags, own_tags, t_send.at[n], t_recv.at[n], device))

    def hand_over(n, rq):
        chunk = spot(n, rq)
        launch(remote(chunk, chunk, h_send.at[n * 4 + rq], h_recv.at[n * 4 + rq], to_sib))

    def arrived(n, rq):
        chunk = spot(n, rq)
        remote(chunk, chunk, g_send.at[0], g_recv.at[n * 4 + rq], to_sib).wait_recv()

    for rq in range(4):
        hand_over(0, rq)
    for copy in w_copies + small_copies[2:]:
        copy.wait()
    w_swap = remote(w.at[1 - core], wsib, e_send.at[0], e_recv.at[0], to_sib)
    launch(w_swap)

    for n in (4, 1, 2, 3, 5, 6, 7):
        arrived(n, 0)
        chunk = spot(n, 0)
        for device, rq, skipped in ((to_twin, 2, (1, 2)), (to_above, 3, (2, 4)), (to_below, 1, (1, 4))):
            if n not in skipped:
                launch(remote(chunk, chunk, g_send.at[next(free_sends)], g_recv.at[n * 4 + rq], device))
        if n == 4:
            post((1, 2, 4), (1,))
        if n == 3:
            post((1, 2, 4), (2,))
        hand_over(n, 0)
    for n in range(1, 8):
        there = tags_ref.at[core, (xh if n < 4 else other) * 4 + (y, up, down, far)[n % 4]]
        remote(there, there, t_send.at[n], t_recv.at[n], to_sib).wait_recv()
    launch(remote(tags_ref.at[core], tags_ref.at[core], t_send.at[0], t_recv.at[0], to_sib))
    for n in (4, 1, 2, 3, 5, 6, 7):
        for rq in (2, 3, 1):
            arrived(n, rq)
            hand_over(n, rq)

    tokens = GROUPS * TOK
    deep = min(512, quad)
    per_half = half // deep
    per_quad = quad // deep

    share = tokens // 2

    def logits_of(c):
        rows = pl.ds(pl.multiple_of(c * share, share), share)
        for b in range(voc // TAG):
            logit[rows, pl.ds(b * TAG, TAG)] = jnp.broadcast_to(bias_ref[b : b + 1, :], (share, TAG))

        def step(q, carry):
            a = hid[c, :, q].reshape(share, quad)
            logit[rows, :] += dot(a, w[q // 2, pl.ds(pl.multiple_of((q % 2) * quad, quad), quad), :])
            return carry

        lax.fori_loop(0, 4, step, 0)

    logits_of(core)

    remote(tags_ref.at[1 - core], tags_ref.at[1 - core], t_send.at[0], t_recv.at[0], to_sib).wait_recv()
    for n in range(8):
        for rq in range(4):
            chunk = spot(n, rq, 1 - core)
            remote(chunk, chunk, h_send.at[0], h_recv.at[n * 4 + rq], to_sib).wait_recv()

    logits_of(1 - core)

    tags = tags_ref[...].reshape(tokens, TAG).astype(F32)
    row = iota((tokens, TAG), 0)
    lane = iota((tokens, TAG), 1)
    index = lane % 32
    wanted_group = index // 2
    wanted_tag = index % 2 + 2 * (lane // 32)
    belongs = (
        (2 * ((row % share) // TOK) + row // share == wanted_group)
        & (tags == wanted_tag.astype(F32))
        & (tags < SEQ_GROUP)
        & (lane < 64)
    )
    member_t = jnp.where(belongs, 1.0, 0.0)
    for i in range(3):
        mt[:, pl.ds(i * TAG, TAG)] = member_t.astype(BF16)
    member = jnp.transpose(member_t)
    inv_count = 1.0 / jnp.maximum(jnp.sum(member, axis=1, keepdims=True), 1.0)
    member = member.astype(BF16)

    def excess_step(i, carry):
        rows = pl.ds(pl.multiple_of(i * TOK, TOK), TOK)
        l = logit[rows, :]
        soft = jnp.maximum(l, 0.0) + jnp.log1p(jnp.exp(-jnp.abs(l)))
        u = 1.0 + jnp.log1p(soft)
        u2 = u * u
        excess[rows, :] = u2 * u2 - 1.0
        return carry

    lax.fori_loop(0, GROUPS, excess_step, 0)
    e1, e2, e3 = split3(excess[...])
    pooled_sum = (dot(member, e1) + dot(member, e2) + dot(member, e3)) * inv_count
    pooled = jnp.log1p(pooled_sum) * 0.25

    wide = iota((32, TAG), 1)
    in_passages = (wide >= 32) & (wide < 64)
    inner = dot(pooled[:32], pooled, ((1,), (1,)), precise)
    inner = jnp.where(in_passages, inner, 0.0)
    packed = inner[0:8]
    packed = pltpu.roll(packed, 96, 1)
    for b in range(1, 4):
        shift = 32 * (b - 1)
        piece = inner[8 * b : 8 * b + 8]
        packed = packed + (pltpu.roll(piece, shift, 1) if shift else piece)
    squares = dot(jnp.ones((8, voc), F32), pooled * pooled, ((1,), (1,)), precise)

    slot = core * DEPTH + z
    ara[slot, 0:8, :] = packed
    ara[slot, 8:9, :] = squares[0:1]
    message = pl.ds(0, 9)
    a_copies = [
        remote(ara.at[slot, message], ara.at[slot, message], a_send.at[k], a_recv.at[k], column_mate(k))
        for k in range(1, PAIR)
    ]
    for copy in a_copies:
        launch(copy)

    def factor_step(i, carry):
        rows = pl.ds(pl.multiple_of(i * TOK, TOK), TOK)
        l = logit[rows, :]
        e = jnp.exp(-jnp.abs(l))
        soft = jnp.maximum(l, 0.0) + jnp.log1p(e)
        u = 1.0 + jnp.log1p(soft)
        top = jnp.where(l >= 0.0, 1.0, e)
        fac[rows, :] = 4.0 * (u * u * u) * top / ((1.0 + e) * (1.0 + soft))
        return carry

    lax.fori_loop(0, GROUPS, factor_step, 0)

    for copy in a_copies:
        copy.wait_recv()
    column_sum = ara[0, message]
    for k in range(1, PAIR):
        column_sum = column_sum + ara[k, message]
    slot_b = x * SIDE + y
    arb[slot_b, message] = column_sum
    b_copies = [
        remote(arb.at[slot_b, message], arb.at[slot_b, message], b_send.at[k], b_recv.at[k], plane_mate(k))
        for k in range(1, PAIR)
    ]
    for copy in b_copies:
        launch(copy)
    for copy in b_copies:
        copy.wait_recv()
    total = arb[0, message]
    for k in range(1, PAIR):
        total = total + arb[k, message]

    pieces = []
    for b in range(4):
        shift = (32 - 32 * b) % 128
        pieces.append(pltpu.roll(total[0:8], shift, 1) if shift else total[0:8])
    inner = jnp.where(in_passages, jnp.concatenate(pieces, axis=0), 0.0)
    square_row = total[8:9]
    eye_wide = iota((TAG, TAG), 0) == iota((TAG, TAG), 1)
    square_col = jnp.sum(jnp.where(eye_wide, jnp.broadcast_to(square_row, (TAG, TAG)), 0.0), axis=1, keepdims=True)
    norm_row = jnp.sqrt(square_row + norm_eps)
    norm_col = jnp.sqrt(square_col + norm_eps)
    cosine = inner / (norm_col[:32] * norm_row)
    scores = score_scale * cosine
    exp_scores = jnp.where(in_passages, jnp.exp(scores), 0.0)
    totals = jnp.sum(exp_scores, axis=0, keepdims=True)
    totals = jnp.where(in_passages[0:1], totals, 1.0)
    labels = labels_ref[...].astype(F32)
    label_col = jnp.sum(jnp.where(eye, jnp.broadcast_to(labels, (32, 32)), 0.0), axis=1, keepdims=True)
    row_id = iota((32, TAG), 0)
    label_row = jnp.sum(
        jnp.where(wide - 32 == row_id, jnp.broadcast_to(label_col, (32, TAG)), 0.0), axis=0, keepdims=True
    )
    chosen = jnp.where((row_id.astype(F32) == label_row) & in_passages, 1.0, 0.0)
    per_passage = jnp.log(totals) - jnp.sum(chosen * scores, axis=0, keepdims=True)
    loss_ref[...] = jnp.sum(per_passage, axis=1, keepdims=True) / 32.0
    score_grad = (loss_scale * score_scale / 32.0) * (exp_scores / totals - chosen)
    blank = jnp.zeros((TAG - 32, TAG), F32)
    grad_full = jnp.concatenate([score_grad, blank], axis=0)
    cos_full = jnp.concatenate([cosine, blank], axis=0)
    grad_sym = grad_full + jnp.transpose(grad_full)
    cos_sym = cos_full + jnp.transpose(cos_full)
    radial = jnp.sum(grad_sym * cos_sym, axis=1, keepdims=True)
    inv_norm = 1.0 / norm_col
    unit = pooled * inv_norm
    pooled_grad = (dot(grad_sym, unit, precision=precise) - unit * radial) * inv_norm
    sum_grad = pooled_grad * inv_count / (4.0 * (1.0 + pooled_sum))

    thirds = jnp.concatenate(split3(sum_grad), axis=0)
    new, old = iota((128, 128), 0), iota((128, 128), 1)
    source = (new // 32) * 32 + ((new // 2) % 8) * 4 + ((new // 16) % 2) * 2 + new % 2
    shuffle = jnp.where(source == old, 1.0, 0.0).astype(BF16)
    lg_swaps = []
    for i in range(4):
        rows = pl.ds(i * 128, 128)
        g = (dot(mt[rows, :], thirds) * fac[rows, :]).astype(BF16)
        lg[rows, :] = g
        p = dot(shuffle, g).astype(BF16)
        cx, part_of = i % 2, pl.ds((i // 2) * 16, 16)
        for b in range(8):
            lgp[cx * 2 + b % 2, b // 2, part_of] = p[b * 16 : b * 16 + 16]
        box = (pl.ds(cx * 2, 2), slice(None), part_of)
        swap = remote(lgp.at[box], lgs.at[box], e_send.at[1 + i], e_recv.at[1 + i], to_sib)
        launch(swap)
        lg_swaps.append(swap)

    span = half // 2
    side = span // 2

    def ring(o):
        return place((x + (1 - core) * o) % 4, (y + core * o) % 4, core, z)

    def ring_two(o):
        return place((x + core * o) % 4, (y + (1 - core) * o) % 4, core, z)

    def rows_of(ref, o):
        picked = []
        for i in range(4):
            px = (1 - core) * ((x + o) % 4) + core * i
            py = core * ((y + o) % 4) + (1 - core) * i
            picked.append(ref[px, py])
        return jnp.concatenate(picked, axis=0)

    def columns(n):
        return pl.ds(n * side, side)

    def term(rows, weights):
        return dot(rows, weights, ((1,), (1,)))

    def keep(o, n, value):
        part[o, :, :, columns(n)] = value.astype(BF16).reshape(4, 32, side)

    def partial(o, n, mine, theirs):
        keep(o, n, term(mine, w[core, columns(n), :]) + term(theirs, wsib[columns(n), :]))

    plus, minus = ring(1), ring(3)
    mine = rows_of(lgp, 2)
    for n in range(4):
        pre[:, columns(n)] = term(mine, w[core, columns(n), :])
    w_swap.wait_recv()
    for swap in lg_swaps:
        swap.wait_recv()
    theirs = rows_of(lgs, 2)
    fars = []
    for n in range(4):
        keep(2, n, pre[:, columns(n)] + term(theirs, wsib[columns(n), :]))
        copy = remote(part.at[2, :, :, columns(n)], fars_in.at[n], r_send.at[n], r_recv.at[n], (plus, minus)[n % 2])
        launch(copy)
        fars.append(copy)
    mine_up, theirs_up = rows_of(lgp, 1), rows_of(lgs, 1)
    mine_down, theirs_down = rows_of(lgp, 3), rows_of(lgs, 3)
    firsts = []

    def pass_on(o, n, k):
        target, landing = ((plus, fromm) if o == 1 else (minus, fromp))
        copy = remote(part.at[o, :, :, columns(n)], landing.at[n], r_send.at[k], r_recv.at[k], target)
        launch(copy)
        firsts.append(copy)

    for h in range(2):
        left, right = 2 * h, 2 * h + 1
        partial(1, right, mine_up, theirs_up)
        pass_on(1, right, 4 + right)
        partial(3, left, mine_down, theirs_down)
        pass_on(3, left, 4 + left)
        partial(1, left, mine_up, theirs_up)
        partial(3, right, mine_down, theirs_down)
        for n, o in ((left, 1), (right, 3)):
            fars[n].wait_recv()
            value = part[o, :, :, columns(n)].astype(F32) + fars_in[n].astype(F32)
            part[o, :, :, columns(n)] = value.astype(BF16)
            pass_on(o, n, 8 + n)
    mine, theirs = rows_of(lgp, 0), rows_of(lgs, 0)
    for n in range(4):
        partial(0, n, mine, theirs)

    def weight_step(i, carry):
        start = pl.multiple_of((i % per_quad) * deep, deep)
        a = hid[:, :, i // per_quad, :, pl.ds(start, deep)].reshape(tokens, deep)
        wgrad_ref[pl.ds(pl.multiple_of(i * deep, deep), deep), :] = dot(a, lg[...], ((0,), (0,))).astype(BF16)
        return carry

    seat = core * x + (1 - core) * y
    seconds = []
    for h in range(2):
        lax.fori_loop(h * per_half, (h + 1) * per_half, weight_step, 0)
        for copy in firsts[4 * h : 4 * h + 4]:
            copy.wait_recv()
        for o in (2, 1, 3, 0):
            i = (seat + o) % 4
            for n in (2 * h, 2 * h + 1):
                cols = columns(n)
                value = part[0, i, :, cols].astype(F32) + fromm[n, i].astype(F32) + fromp[n, i].astype(F32)
                acc[h, i, :, pl.ds((n % 2) * side, side)] = value.astype(BF16)
            if o:
                k = h * 3 + o - 1
                copy = remote(acc.at[h, i], rtwo.at[k], s_send.at[k], s_recv.at[k], ring_two(o))
                launch(copy)
                seconds.append(copy)
    wg_copy = pltpu.make_async_copy(wgrad_ref, wgrad_hbm, loc_sem.at[10])
    wg_copy.start()

    slab = span // 8
    new, old = iota((256, 256), 0), iota((256, 256), 1)
    source = (new % 8) * 32 + (new // 16) * 2 + (new // 8) % 2
    shuffle = jnp.where(source == old, 1.0, 0.0).astype(BF16)
    lasts = []
    for h in range(2):
        for copy in seconds[3 * h : 3 * h + 3]:
            copy.wait_recv()
        rows = acc[h, seat].astype(F32)
        for o in range(3):
            rows = rows + rtwo[h * 3 + o].astype(F32)
        rows = rows.astype(BF16)
        stacked = jnp.concatenate([rows[:, b * slab : (b + 1) * slab] for b in range(8)], axis=0)
        zsend[h] = dot(shuffle, stacked).astype(BF16).reshape(16, 16, slab)
        for k in range(1, PAIR):
            target = ((core + k // DEPTH) % 2) * DEPTH + (z + k % DEPTH) % DEPTH
            sem = h * PAIR + k
            copy = remote(zsend.at[h, target], zrecv.at[h, slot], z_send.at[sem], z_recv.at[sem], column_mate(k))
            launch(copy)
            lasts.append(copy)
        zrecv[h, slot] = zsend[h, slot]
    for h in range(2):
        for copy in lasts[15 * h : 15 * h + 15]:
            copy.wait_recv()
        for c in range(2):
            value = zrecv[h, c * DEPTH].astype(F32)
            for k in range(1, DEPTH):
                value = value + zrecv[h, c * DEPTH + k].astype(F32)
            for r in range(2):
                for b in range(8):
                    cols = pl.ds(c * half + h * span + b * slab, slab)
                    hgrad_ref[r : r + 1, cols] = value[r * 8 + b : r * 8 + b + 1]

    wg_copy.wait()
    for copy in sent:
        copy.wait_send()


def finish(loss_in, wgrad_in, hgrad_in, loss_out, wgrad_out, hgrad_out, loss, wgrad, hgrad, load_sem, store_sem):
    step = wgrad.shape[0] // CHUNKS
    stages = [(hgrad_in, hgrad, hgrad_out), (loss_in, loss, loss_out)]
    for i in range(CHUNKS):
        rows = pl.ds(i * step, step)
        stages.append((wgrad_in.at[rows, :], wgrad.at[rows, :], wgrad_out.at[rows, :]))
    loads = [pltpu.make_async_copy(src, via, load_sem.at[i]) for i, (src, via, _) in enumerate(stages)]
    stores = [pltpu.make_async_copy(via, dst, store_sem.at[i]) for i, (_, via, dst) in enumerate(stages)]
    for copy in loads:
        copy.start()
    for load, store in zip(loads, stores):
        load.wait()
        store.start()
    for copy in stores:
        copy.wait()


def body(hidden, head_weight, vocab_bias, seq_ids, token_mask, labels):
    width, voc = head_weight.shape
    half = width // 2
    tokens = GROUPS * TOK
    vmem = pl.BlockSpec(memory_space=pltpu.VMEM)
    hbm = pl.BlockSpec(memory_space=pltpu.HBM)
    dma = pltpu.SemaphoreType.DMA
    shapes = (
        jax.ShapeDtypeStruct((1, 1), F32),
        jax.ShapeDtypeStruct((width, voc), BF16),
        jax.ShapeDtypeStruct((2, width), F32),
    )
    results = pl.pallas_call(
        fused,
        out_shape=shapes,
        in_specs=[hbm] * 6,
        out_specs=(vmem, hbm, vmem),
        scratch_shapes=[
            pltpu.VMEM((voc // TAG, TAG), F32),
            pltpu.VMEM((1, TOK), jnp.int32),
            pltpu.VMEM((1, TOK), jnp.int32),
            pltpu.VMEM((1, 32), jnp.int32),
            pltpu.VMEM((width, voc), BF16),
            pltpu.VMEM((2, GROUPS // 2, 4, TOK, width // 4), BF16),
            pltpu.VMEM((2, GROUPS // 2, TOK, TAG), BF16),
            pltpu.VMEM((2, half, voc), BF16),
            pltpu.VMEM((half, voc), BF16),
            pltpu.VMEM((tokens, voc), F32),
            pltpu.VMEM((tokens, voc), F32),
            pltpu.VMEM((tokens, voc), F32),
            pltpu.VMEM((tokens, 3 * TAG), BF16),
            pltpu.VMEM((tokens, voc), BF16),
            pltpu.VMEM((4, 4, TOK, voc), BF16),
            pltpu.VMEM((4, 4, TOK, voc), BF16),
            pltpu.VMEM((PAIR, 16, TAG), F32),
            pltpu.VMEM((PAIR, 16, TAG), F32),
            pltpu.VMEM((4 * TOK, half), F32),
            pltpu.VMEM((4, 4, TOK, half), BF16),
            pltpu.VMEM((4, 4, TOK, half // 4), BF16),
            pltpu.VMEM((4, 4, TOK, half // 4), BF16),
            pltpu.VMEM((4, 4, TOK, half // 4), BF16),
            pltpu.VMEM((2, 4, TOK, half // 2), BF16),
            pltpu.VMEM((6, TOK, half // 2), BF16),
            pltpu.VMEM((2, PAIR, 16, half // 16), BF16),
            pltpu.VMEM((2, PAIR, 16, half // 16), BF16),
            dma((11,)),
            dma((GATHER_COPIES,)),
            dma((32,)),
            dma((32,)),
            dma((32,)),
            dma((8,)),
            dma((8,)),
            dma((5,)),
            dma((5,)),
            dma((PAIR,)),
            dma((PAIR,)),
            dma((PAIR,)),
            dma((PAIR,)),
            dma((12,)),
            dma((12,)),
            dma((6,)),
            dma((6,)),
            dma((2 * PAIR,)),
            dma((2 * PAIR,)),
        ],
        compiler_params=pltpu.CompilerParams(
            collective_id=0, has_side_effects=True, vmem_limit_bytes=60 * 1024 * 1024
        ),
        name="splade_head",
    )(
        hidden,
        head_weight,
        vocab_bias.reshape(voc // TAG, TAG),
        seq_ids,
        token_mask,
        labels.reshape(1, labels.shape[0]),
    )
    loss, weight_grad, hidden_grad = pl.pallas_call(
        finish,
        out_shape=shapes,
        in_specs=[hbm] * 3,
        out_specs=(hbm,) * 3,
        scratch_shapes=[
            *(pltpu.VMEM(shape.shape, shape.dtype) for shape in shapes),
            dma((CHUNKS + 2,)),
            dma((CHUNKS + 2,)),
        ],
        compiler_params=pltpu.CompilerParams(vmem_limit_bytes=60 * 1024 * 1024),
        name="results",
    )(*results)
    return loss.reshape(()), weight_grad, hidden_grad


def solution(mesh):
    in_specs = (
        P("dp", None),
        P(None, ("dp", "vocab")),
        P(("dp", "vocab")),
        P("dp", None),
        P("dp", None),
        P(),
    )
    out_specs = (P(), P(None, ("dp", "vocab")), P(("dp", "vocab"), None))
    return jax.shard_map(body, mesh=mesh, in_specs=in_specs, out_specs=out_specs, check_vma=False)
```

```python
import functools

import jax
import jax.numpy as jnp
from jax import lax
from jax.experimental import pallas as pl
from jax.experimental.pallas import tpu as pltpu
from jax.sharding import PartitionSpec as P

MESH = pl.DeviceIdType.MESH
F32, BF16 = jnp.float32, jnp.bfloat16

SEQ_GROUP = 4
GROUPS = 16
TOK = 32
SIDE = 4
DEPTH = 8
TAG = 128

score_scale = 20.0
loss_scale = 65536.0
norm_eps = 1e-06
precise = lax.Precision.HIGHEST

PAIR = 16
CHUNKS = 8


def iota(shape, dim):
    return lax.broadcasted_iota(jnp.int32, shape, dim)


def split3(x):
    first = x.astype(BF16)
    rest = x - first.astype(F32)
    second = rest.astype(BF16)
    third = (rest - second.astype(F32)).astype(BF16)
    return first, second, third


def dot(a, b, dims=((1,), (0,)), precision=None):
    return lax.dot_general(a, b, (dims, ((), ())), precision=precision, preferred_element_type=F32)


def fused(
    hidden_ref, weight_ref, bias_hbm, seq_hbm, mask_hbm, labels_hbm,
    loss_hbm, wgrad_hbm, hgrad_hbm,
    loss_ref, hgrad_ref, bias_ref, seq_ref, mask_ref, labels_ref, wgrad_ref,
    hid, tags_ref, w, wsib, logit, fac, excess, mt, lg, lgp, lgs,
    pooled_six, sum_scale, ara, arb, pre, part, fars_in, fromm, fromp, acc, rtwo, zsend, zrecv,
    loc_sem, g_send, g_recv, h_send, h_recv, t_send, t_recv, e_send, e_recv, a_send, a_recv, b_send, b_recv,
    r_send, r_recv, s_send, s_recv, z_send, z_recv,
):
    width = hidden_ref.shape[1]
    half = width // 2
    voc = weight_ref.shape[1]
    d, v = lax.axis_index("dp"), lax.axis_index("vocab")
    core, y, xh = d % 2, (d // 2) % 4, d // 8
    xl, z = v % 2, v // 2
    x = xh * 2 + xl

    def place(px, py, pc, pz):
        return ((px // 2) * 8 + py * 2 + pc, pz * 2 + px % 2)

    def column_mate(k):
        return place(x, y, (core + k // DEPTH) % 2, (z + k % DEPTH) % DEPTH)

    def plane_mate(k):
        return place((x + k // SIDE) % SIDE, (y + k % SIDE) % SIDE, core, z)

    def remote(src, dst, send, recv, device):
        return pltpu.make_async_remote_copy(
            src_ref=src, dst_ref=dst, send_sem=send, recv_sem=recv, device_id=device, device_id_type=MESH
        )

    def all_sent(source, sem):
        remote(source, source, sem, sem, to_sib).wait_send()

    def all_here(target, sem):
        remote(target, target, sem, sem, to_sib).wait_recv()

    to_sib = place(x, y, 1 - core, z)

    w_copies = [
        pltpu.make_async_copy(weight_ref.at[pl.ds(h * half, half), :], w.at[h], loc_sem.at[h]) for h in range(2)
    ]
    quad = width // 4
    seat_t = xh * 4 + y
    h_copies = [
        pltpu.make_async_copy(hidden_ref.at[:, pl.ds(q * quad, quad)], hid.at[core, seat_t, q], loc_sem.at[2 + q])
        for q in range(4)
    ]
    small_copies = [
        pltpu.make_async_copy(src, dst, loc_sem.at[6 + i])
        for i, (src, dst) in enumerate(
            ((seq_hbm, seq_ref), (mask_hbm, mask_ref), (bias_hbm, bias_ref), (labels_hbm, labels_ref))
        )
    ]
    for copy in small_copies[:2] + h_copies + w_copies + small_copies[2:]:
        copy.start()

    barrier = pltpu.get_barrier_semaphore()
    for k in (2, 1, 3):
        pl.semaphore_signal(barrier, inc=1, device_id=plane_mate(k), device_id_type=MESH)
    for k in (1, 7, 8):
        pl.semaphore_signal(barrier, inc=1, device_id=column_mate(k), device_id_type=MESH)
    for k in range(4, PAIR):
        pl.semaphore_signal(barrier, inc=1, device_id=plane_mate(k), device_id_type=MESH)
    for k in (2, 3, 4, 5, 6, 9, 10, 11, 12, 13, 14, 15):
        pl.semaphore_signal(barrier, inc=1, device_id=column_mate(k), device_id_type=MESH)

    eye = iota((TOK, TOK), 0) == iota((TOK, TOK), 1)
    for copy in small_copies[:2]:
        copy.wait()
    tag_row = jnp.where(mask_ref[...] > 0, seq_ref[...], SEQ_GROUP).astype(F32)
    tag_col = jnp.sum(jnp.where(eye, jnp.broadcast_to(tag_row, (TOK, TOK)), 0.0), axis=1, keepdims=True)
    tags_ref[core, seat_t] = jnp.broadcast_to(tag_col, (TOK, TAG)).astype(BF16)
    pl.semaphore_wait(barrier, 2 * (PAIR - 1))

    up, down, far = (y + 1) % 4, (y + 3) % 4, (y + 2) % 4
    other = 1 - xh
    cross_x = other * 2 + 1 - xl
    colour = (z + 2 * xl) % 4
    to_twin = place(xh * 2 + 1 - xl, y, core, z)
    to_above = place(x, y, core, (z + 1) % DEPTH)
    to_below = place(x, y, core, (z + DEPTH - 1) % DEPTH)

    def spot(n, rq, of_core=core):
        row = (xh if n < 4 else other) * 4 + (y, up, down, far)[n % 4]
        return hid.at[of_core, row, (colour + rq) % 4]

    fetches = (
        (place(cross_x, y, core, z), 4, 2, (0, 1, 3)),
        (place(x, down, core, z), 1, 0, (0, 2, 1)),
        (place(x, up, core, z), 2, 0, (0, 2, 3)),
        (place(x, far, core, z), 3, 0, (0,)),
        (place(cross_x, down, core, z), 5, 2, (0,)),
        (place(cross_x, up, core, z), 6, 2, (0,)),
        (place(cross_x, far, core, z), 7, 2, (0,)),
    )
    def post(chunks, levels):
        for level in levels:
            for device, n, shift, quarters in fetches:
                if n in chunks and level < len(quarters):
                    rq = quarters[level]
                    q = (colour + shift + rq) % 4
                    src = hid.at[core, seat_t, q]
                    remote(src, src, g_send, g_recv.at[n * 4 + rq], device).start()

    for copy in h_copies:
        copy.wait()
    post((1, 2, 3, 4, 5, 6, 7), (0,))
    own_tags = tags_ref.at[core, seat_t]
    for device, n, _, _ in fetches:
        remote(own_tags, own_tags, t_send.at[0], t_recv.at[n], device).start()

    def hand_over(n, rq):
        chunk = spot(n, rq)
        remote(chunk, chunk, h_send, h_recv.at[n], to_sib).start()

    def arrived(n, rq):
        chunk = spot(n, rq)
        all_here(chunk, g_recv.at[n * 4 + rq])

    for rq in range(4):
        hand_over(0, rq)
    for copy in w_copies + small_copies[2:]:
        copy.wait()
    w_swap = remote(w.at[1 - core], wsib, e_send.at[0], e_recv.at[0], to_sib)
    w_swap.start()

    for n in (4, 1, 2, 3, 5, 6, 7):
        arrived(n, 0)
        chunk = spot(n, 0)
        for device, rq, skipped in ((to_twin, 2, (1, 2)), (to_above, 3, (2, 4)), (to_below, 1, (1, 4))):
            if n not in skipped:
                remote(chunk, chunk, g_send, g_recv.at[n * 4 + rq], device).start()
        if n == 4:
            post((1, 2, 4), (1,))
        if n == 3:
            post((1, 2, 4), (2,))
        hand_over(n, 0)
    for n in range(1, 8):
        there = tags_ref.at[core, (xh if n < 4 else other) * 4 + (y, up, down, far)[n % 4]]
        all_here(there, t_recv.at[n])
    remote(tags_ref.at[core], tags_ref.at[core], t_send.at[1], t_recv.at[0], to_sib).start()
    tokens = GROUPS * TOK
    deep = min(512, quad)
    per_half = half // deep
    per_quad = quad // deep
    share = tokens // 2

    def logits_of(c, rows_x):
        rows = pl.ds(pl.multiple_of(c * share + rows_x * 128, 128), 128)
        for b in range(voc // TAG):
            logit[rows, pl.ds(b * TAG, TAG)] = jnp.broadcast_to(bias_ref[b : b + 1, :], (128, TAG))

        def step(q, carry):
            a = hid[c, pl.ds(rows_x * 4, 4), q].reshape(128, quad)
            logit[rows, :] += dot(a, w[q // 2, pl.ds(pl.multiple_of((q % 2) * quad, quad), quad), :])
            return carry

        lax.fori_loop(0, 4, step, 0)

        def excess_step(i, carry):
            rows = pl.ds(pl.multiple_of(c * share + rows_x * 128 + i * TOK, TOK), TOK)
            l = logit[rows, :]
            soft = jnp.maximum(l, 0.0) + jnp.log1p(jnp.exp(-jnp.abs(l)))
            u = 1.0 + jnp.log1p(soft)
            u2 = u * u
            excess[rows, :] = u2 * u2 - 1.0
            return carry

        lax.fori_loop(0, 4, excess_step, 0)

    def complete(chunks):
        for n in chunks:
            for rq in (2, 3, 1):
                arrived(n, rq)
                hand_over(n, rq)

    def handed(chunks):
        for n in chunks:
            row = (xh if n < 4 else other) * 4 + (y, up, down, far)[n % 4]
            all_here(hid.at[1 - core, row], h_recv.at[n])

    complete((1, 2, 3))
    logits_of(core, xh)
    complete((4, 5, 6, 7))
    logits_of(core, other)
    handed((0, 1, 2, 3))
    logits_of(1 - core, xh)
    handed((4, 5, 6, 7))
    logits_of(1 - core, other)
    all_here(tags_ref.at[1 - core], t_recv.at[0])

    tags = tags_ref[...].reshape(tokens, TAG).astype(F32)
    row = iota((tokens, TAG), 0)
    lane = iota((tokens, TAG), 1)
    index = lane % 32
    wanted_group = index // 2
    wanted_tag = index % 2 + 2 * (lane // 32)
    belongs = (
        (2 * ((row % share) // TOK) + row // share == wanted_group)
        & (tags == wanted_tag.astype(F32))
        & (tags < SEQ_GROUP)
        & (lane < 64)
    )
    member_t = jnp.where(belongs, 1.0, 0.0)
    for i in range(3):
        mt[:, pl.ds(i * TAG, TAG)] = member_t.astype(BF16)
    member = jnp.transpose(member_t)
    inv_count = 1.0 / jnp.maximum(jnp.sum(member, axis=1, keepdims=True), 1.0)
    member = member.astype(BF16)

    e1, e2, e3 = split3(excess[...])
    pooled_sum = (dot(member, e1) + dot(member, e2) + dot(member, e3)) * inv_count
    pooled = jnp.log1p(pooled_sum) * 0.25
    p1, p2, p3 = split3(pooled)
    for i, piece in enumerate((p1, p2, p1, p3, p2, p1)):
        pooled_six[pl.ds(i * TAG, TAG), :] = piece
    sum_scale[...] = inv_count / (4.0 * (1.0 + pooled_sum))

    wide = iota((32, TAG), 1)
    in_passages = (wide >= 32) & (wide < 64)
    inner = dot(pooled[:32], pooled, ((1,), (1,)), precise)
    inner = jnp.where(in_passages, inner, 0.0)
    packed = inner[0:8]
    packed = pltpu.roll(packed, 96, 1)
    for b in range(1, 4):
        shift = 32 * (b - 1)
        piece = inner[8 * b : 8 * b + 8]
        packed = packed + (pltpu.roll(piece, shift, 1) if shift else piece)
    squares = dot(jnp.ones((8, voc), F32), pooled * pooled, ((1,), (1,)), precise)

    slot = core * DEPTH + z
    ara[slot, 0:8, :] = packed
    ara[slot, 8:9, :] = squares[0:1]
    message = pl.ds(0, 9)
    mail = ara.at[slot, message]
    for k in range(1, PAIR):
        remote(mail, mail, a_send, a_recv, column_mate(k)).start()

    def factor_step(i, carry):
        rows = pl.ds(pl.multiple_of(i * TOK, TOK), TOK)
        l = logit[rows, :]
        e = jnp.exp(-jnp.abs(l))
        soft = jnp.maximum(l, 0.0) + jnp.log1p(e)
        u = 1.0 + jnp.log1p(soft)
        top = jnp.where(l >= 0.0, 1.0, e)
        fac[rows, :] = 4.0 * (u * u * u) * top / ((1.0 + e) * (1.0 + soft))
        return carry

    lax.fori_loop(0, GROUPS, factor_step, 0)

    all_here(ara.at[pl.ds(1, PAIR - 1), message], a_recv)
    column_sum = ara[0, message]
    for k in range(1, PAIR):
        column_sum = column_sum + ara[k, message]
    slot_b = x * SIDE + y
    arb[slot_b, message] = column_sum
    mail = arb.at[slot_b, message]
    for k in range(1, PAIR):
        remote(mail, mail, b_send, b_recv, plane_mate(k)).start()
    all_sent(hid.at[0, pl.ds(0, 7)], g_send)
    all_sent(hid.at[0], h_send)
    all_sent(tags_ref.at[0, pl.ds(0, 7)], t_send.at[0])
    all_sent(tags_ref.at[0], t_send.at[1])
    all_sent(ara.at[pl.ds(1, PAIR - 1), message], a_send)
    all_here(arb.at[pl.ds(1, PAIR - 1), message], b_recv)
    total = arb[0, message]
    for k in range(1, PAIR):
        total = total + arb[k, message]

    pieces = []
    for b in range(4):
        shift = (32 - 32 * b) % 128
        pieces.append(pltpu.roll(total[0:8], shift, 1) if shift else total[0:8])
    inner = jnp.where(in_passages, jnp.concatenate(pieces, axis=0), 0.0)
    square_row = total[8:9]
    eye_wide = iota((TAG, TAG), 0) == iota((TAG, TAG), 1)
    square_col = jnp.sum(jnp.where(eye_wide, jnp.broadcast_to(square_row, (TAG, TAG)), 0.0), axis=1, keepdims=True)
    norm_row = jnp.sqrt(square_row + norm_eps)
    norm_col = jnp.sqrt(square_col + norm_eps)
    cosine = inner / (norm_col[:32] * norm_row)
    scores = score_scale * cosine
    exp_scores = jnp.where(in_passages, jnp.exp(scores), 0.0)
    totals = jnp.sum(exp_scores, axis=0, keepdims=True)
    totals = jnp.where(in_passages[0:1], totals, 1.0)
    labels = labels_ref[...].astype(F32)
    label_col = jnp.sum(jnp.where(eye, jnp.broadcast_to(labels, (32, 32)), 0.0), axis=1, keepdims=True)
    row_id = iota((32, TAG), 0)
    label_row = jnp.sum(
        jnp.where(wide - 32 == row_id, jnp.broadcast_to(label_col, (32, TAG)), 0.0), axis=0, keepdims=True
    )
    chosen = jnp.where((row_id.astype(F32) == label_row) & in_passages, 1.0, 0.0)
    per_passage = jnp.log(totals) - jnp.sum(chosen * scores, axis=0, keepdims=True)
    score_grad = (loss_scale * score_scale / 32.0) * (exp_scores / totals - chosen)
    blank = jnp.zeros((TAG - 32, TAG), F32)
    grad_full = jnp.concatenate([score_grad, blank], axis=0)
    cos_full = jnp.concatenate([cosine, blank], axis=0)
    grad_sym = grad_full + jnp.transpose(grad_full)
    cos_sym = cos_full + jnp.transpose(cos_full)
    radial = jnp.sum(grad_sym * cos_sym, axis=1, keepdims=True)
    inv_col, inv_row = 1.0 / norm_col, 1.0 / norm_row
    mix = inv_col * (grad_sym * inv_row - jnp.where(eye_wide, radial * inv_col, 0.0))
    m1, m2, m3 = split3(mix)
    sum_grad = dot(jnp.concatenate([m1, m1, m2, m1, m2, m3], axis=1), pooled_six[...]) * sum_scale[...]

    thirds = jnp.concatenate(split3(sum_grad), axis=0)
    new, old = iota((128, 128), 0), iota((128, 128), 1)
    source = (new // 32) * 32 + ((new // 2) % 8) * 4 + ((new // 16) % 2) * 2 + new % 2
    shuffle = jnp.where(source == old, 1.0, 0.0).astype(BF16)
    lg_swaps = []
    for i in range(4):
        rows = pl.ds(i * 128, 128)
        g = (dot(mt[rows, :], thirds) * fac[rows, :]).astype(BF16)
        lg[rows, :] = g
        p = dot(shuffle, g).astype(BF16)
        cx, part_of = i % 2, pl.ds((i // 2) * 16, 16)
        for b in range(8):
            lgp[cx * 2 + b % 2, b // 2, part_of] = p[b * 16 : b * 16 + 16]
        box = (pl.ds(cx * 2, 2), slice(None), part_of)
        swap = remote(lgp.at[box], lgs.at[box], e_send.at[1 + i], e_recv.at[1 + i], to_sib)
        swap.start()
        lg_swaps.append(swap)

    loss_ref[...] = jnp.sum(per_passage, axis=1, keepdims=True) / 32.0

    span = half // 2
    side = span // 2

    def ring(o):
        return place((x + (1 - core) * o) % 4, (y + core * o) % 4, core, z)

    def ring_two(o):
        return place((x + core * o) % 4, (y + (1 - core) * o) % 4, core, z)

    def rows_of(ref, o):
        picked = []
        for i in range(4):
            px = (1 - core) * ((x + o) % 4) + core * i
            py = core * ((y + o) % 4) + (1 - core) * i
            picked.append(ref[px, py])
        return jnp.concatenate(picked, axis=0)

    def columns(n):
        return pl.ds(n * side, side)

    def term(rows, weights):
        return dot(rows, weights, ((1,), (1,)))

    def keep(o, n, value):
        part[o, :, :, columns(n)] = value.astype(BF16).reshape(4, 32, side)

    def partial(o, n, mine, theirs):
        keep(o, n, term(mine, w[core, columns(n), :]) + term(theirs, wsib[columns(n), :]))

    plus, minus = ring(1), ring(3)
    mine = rows_of(lgp, 2)
    for n in range(4):
        pre[:, columns(n)] = term(mine, w[core, columns(n), :])
    w_swap.wait_recv()
    for swap in lg_swaps:
        swap.wait_recv()
    theirs = rows_of(lgs, 2)
    fars = []
    for n in range(4):
        keep(2, n, pre[:, columns(n)] + term(theirs, wsib[columns(n), :]))
        copy = remote(part.at[2, :, :, columns(n)], fars_in.at[n], r_send, r_recv.at[n], (plus, minus)[n % 2])
        copy.start()
        fars.append(copy)
    mine_up, theirs_up = rows_of(lgp, 1), rows_of(lgs, 1)
    mine_down, theirs_down = rows_of(lgp, 3), rows_of(lgs, 3)
    firsts = []

    def pass_on(o, n, k):
        target, landing = ((plus, fromm) if o == 1 else (minus, fromp))
        copy = remote(part.at[o, :, :, columns(n)], landing.at[n], r_send, r_recv.at[k], target)
        copy.start()
        firsts.append(copy)

    for h in range(2):
        left, right = 2 * h, 2 * h + 1
        partial(1, right, mine_up, theirs_up)
        pass_on(1, right, 4 + right)
        partial(3, left, mine_down, theirs_down)
        pass_on(3, left, 4 + left)
        partial(1, left, mine_up, theirs_up)
        partial(3, right, mine_down, theirs_down)
        for n, o in ((left, 1), (right, 3)):
            fars[n].wait_recv()
            value = part[o, :, :, columns(n)].astype(F32) + fars_in[n].astype(F32)
            part[o, :, :, columns(n)] = value.astype(BF16)
            pass_on(o, n, 8 + n)
    mine, theirs = rows_of(lgp, 0), rows_of(lgs, 0)
    for n in range(4):
        partial(0, n, mine, theirs)

    def weight_step(i, carry):
        start = pl.multiple_of((i % per_quad) * deep, deep)
        a = hid[:, :, i // per_quad, :, pl.ds(start, deep)].reshape(tokens, deep)
        wgrad_ref[pl.ds(pl.multiple_of(i * deep, deep), deep), :] = dot(a, lg[...], ((0,), (0,))).astype(BF16)
        return carry

    seat = core * x + (1 - core) * y
    for h in range(2):
        lax.fori_loop(h * per_half, (h + 1) * per_half, weight_step, 0)
        for copy in firsts[4 * h : 4 * h + 4]:
            copy.wait_recv()
        for o in (2, 1, 3, 0):
            i = (seat + o) % 4
            for n in (2 * h, 2 * h + 1):
                cols = columns(n)
                value = part[0, i, :, cols].astype(F32) + fromm[n, i].astype(F32) + fromp[n, i].astype(F32)
                acc[h, i, :, pl.ds((n % 2) * side, side)] = value.astype(BF16)
            if o:
                k = h * 3 + o - 1
                copy = remote(acc.at[h, i], rtwo.at[k], s_send, s_recv.at[h], ring_two(o))
                copy.start()
    wg_copy = pltpu.make_async_copy(wgrad_ref, wgrad_hbm, loc_sem.at[10])
    wg_copy.start()
    w_swap.wait_send()
    for swap in lg_swaps:
        swap.wait_send()
    all_sent(arb.at[pl.ds(1, PAIR - 1), message], b_send)
    all_sent(part.at[pl.ds(0, 3)], r_send)

    slab = span // 8
    new, old = iota((256, 256), 0), iota((256, 256), 1)
    source = (new % 8) * 32 + (new // 16) * 2 + (new // 8) % 2
    shuffle = jnp.where(source == old, 1.0, 0.0).astype(BF16)
    for h in range(2):
        all_here(rtwo.at[pl.ds(3 * h, 3)], s_recv.at[h])
        rows = acc[h, seat].astype(F32)
        for o in range(3):
            rows = rows + rtwo[h * 3 + o].astype(F32)
        rows = rows.astype(BF16)
        stacked = jnp.concatenate([rows[:, b * slab : (b + 1) * slab] for b in range(8)], axis=0)
        zsend[h] = dot(shuffle, stacked).astype(BF16).reshape(16, 16, slab)
        for k in range(1, PAIR):
            target = ((core + k // DEPTH) % 2) * DEPTH + (z + k % DEPTH) % DEPTH
            remote(zsend.at[h, target], zrecv.at[h, slot], z_send, z_recv.at[h], column_mate(k)).start()
        zrecv[h, slot] = zsend[h, slot]
    all_sent(rtwo, s_send)
    for h in range(2):
        all_here(zrecv.at[h, pl.ds(1, PAIR - 1)], z_recv.at[h])
        for c in range(2):
            value = zrecv[h, c * DEPTH].astype(F32)
            for k in range(1, DEPTH):
                value = value + zrecv[h, c * DEPTH + k].astype(F32)
            for r in range(2):
                for b in range(8):
                    cols = pl.ds(c * half + h * span + b * slab, slab)
                    hgrad_ref[r : r + 1, cols] = value[r * 8 + b : r * 8 + b + 1]

    out_copies = [
        pltpu.make_async_copy(hgrad_ref, hgrad_hbm, loc_sem.at[11]),
        pltpu.make_async_copy(loss_ref, loss_hbm, loc_sem.at[12]),
    ]
    for copy in out_copies:
        copy.start()
    for h in range(2):
        all_sent(zsend.at[h, pl.ds(1, PAIR - 1)], z_send)
    for copy in out_copies:
        copy.wait()
    wg_copy.wait()


def finish(loss_in, wgrad_in, hgrad_in, loss_out, wgrad_out, hgrad_out, loss, wgrad, hgrad, load_sem, store_sem):
    step = wgrad.shape[0] // CHUNKS
    stages = [(hgrad_in, hgrad, hgrad_out), (loss_in, loss, loss_out)]
    for i in range(CHUNKS):
        rows = pl.ds(i * step, step)
        stages.append((wgrad_in.at[rows, :], wgrad.at[rows, :], wgrad_out.at[rows, :]))
    loads = [pltpu.make_async_copy(src, via, load_sem.at[i]) for i, (src, via, _) in enumerate(stages)]
    stores = [pltpu.make_async_copy(via, dst, store_sem.at[i]) for i, (_, via, dst) in enumerate(stages)]
    for copy in loads:
        copy.start()
    for load, store in zip(loads, stores):
        load.wait()
        store.start()
    for copy in stores:
        copy.wait()


def body(hidden, head_weight, vocab_bias, seq_ids, token_mask, labels):
    width, voc = head_weight.shape
    half = width // 2
    tokens = GROUPS * TOK
    hbm = pl.BlockSpec(memory_space=pltpu.HBM)
    dma = pltpu.SemaphoreType.DMA
    shapes = (
        jax.ShapeDtypeStruct((1, 1), F32),
        jax.ShapeDtypeStruct((width, voc), BF16),
        jax.ShapeDtypeStruct((2, width), F32),
    )
    results = pl.pallas_call(
        fused,
        out_shape=shapes,
        in_specs=[hbm] * 6,
        out_specs=(hbm, hbm, hbm),
        scratch_shapes=[
            pltpu.VMEM((1, 1), F32),
            pltpu.VMEM((2, width), F32),
            pltpu.VMEM((voc // TAG, TAG), F32),
            pltpu.VMEM((1, TOK), jnp.int32),
            pltpu.VMEM((1, TOK), jnp.int32),
            pltpu.VMEM((1, 32), jnp.int32),
            pltpu.VMEM((width, voc), BF16),
            pltpu.VMEM((2, GROUPS // 2, 4, TOK, width // 4), BF16),
            pltpu.VMEM((2, GROUPS // 2, TOK, TAG), BF16),
            pltpu.VMEM((2, half, voc), BF16),
            pltpu.VMEM((half, voc), BF16),
            pltpu.VMEM((tokens, voc), F32),
            pltpu.VMEM((tokens, voc), F32),
            pltpu.VMEM((tokens, voc), F32),
            pltpu.VMEM((tokens, 3 * TAG), BF16),
            pltpu.VMEM((tokens, voc), BF16),
            pltpu.VMEM((4, 4, TOK, voc), BF16),
            pltpu.VMEM((4, 4, TOK, voc), BF16),
            pltpu.VMEM((6 * TAG, voc), BF16),
            pltpu.VMEM((TAG, voc), F32),
            pltpu.VMEM((PAIR, 16, TAG), F32),
            pltpu.VMEM((PAIR, 16, TAG), F32),
            pltpu.VMEM((4 * TOK, half), F32),
            pltpu.VMEM((4, 4, TOK, half), BF16),
            pltpu.VMEM((4, 4, TOK, half // 4), BF16),
            pltpu.VMEM((4, 4, TOK, half // 4), BF16),
            pltpu.VMEM((4, 4, TOK, half // 4), BF16),
            pltpu.VMEM((2, 4, TOK, half // 2), BF16),
            pltpu.VMEM((6, TOK, half // 2), BF16),
            pltpu.VMEM((2, PAIR, 16, half // 16), BF16),
            pltpu.VMEM((2, PAIR, 16, half // 16), BF16),
            dma((13,)),
            dma,
            dma((32,)),
            dma,
            dma((8,)),
            dma((2,)),
            dma((8,)),
            dma((5,)),
            dma((5,)),
            dma,
            dma,
            dma,
            dma,
            dma,
            dma((12,)),
            dma,
            dma((2,)),
            dma,
            dma((2,)),
        ],
        compiler_params=pltpu.CompilerParams(
            collective_id=0, has_side_effects=True, vmem_limit_bytes=60 * 1024 * 1024
        ),
        name="splade_head",
    )(
        hidden,
        head_weight,
        vocab_bias.reshape(voc // TAG, TAG),
        seq_ids,
        token_mask,
        labels.reshape(1, labels.shape[0]),
    )
    loss, weight_grad, hidden_grad = pl.pallas_call(
        finish,
        out_shape=shapes,
        in_specs=[hbm] * 3,
        out_specs=(hbm,) * 3,
        scratch_shapes=[
            *(pltpu.VMEM(shape.shape, shape.dtype) for shape in shapes),
            dma((CHUNKS + 2,)),
            dma((CHUNKS + 2,)),
        ],
        compiler_params=pltpu.CompilerParams(vmem_limit_bytes=60 * 1024 * 1024),
        name="results",
    )(*results)
    return loss.reshape(()), weight_grad, hidden_grad


def solution(mesh):
    in_specs = (
        P("dp", None),
        P(None, ("dp", "vocab")),
        P(("dp", "vocab")),
        P("dp", None),
        P("dp", None),
        P(),
    )
    out_specs = (P(), P(None, ("dp", "vocab")), P(("dp", "vocab"), None))
    return jax.shard_map(body, mesh=mesh, in_specs=in_specs, out_specs=out_specs, check_vma=False)
```

```python
import functools

import jax
import jax.numpy as jnp
from jax import lax
from jax.experimental import pallas as pl
from jax.experimental.pallas import tpu as pltpu
from jax.sharding import PartitionSpec as P

MESH = pl.DeviceIdType.MESH
F32, BF16 = jnp.float32, jnp.bfloat16

SEQ_GROUP = 4
GROUPS = 16
TOK = 32
SIDE = 4
DEPTH = 8
TAG = 128

score_scale = 20.0
loss_scale = 65536.0
norm_eps = 1e-06
precise = lax.Precision.HIGHEST

PAIR = 16
CHUNKS = 8
COLUMN_ORDER = (12, 4, 11, 13, 3, 5, 10, 14, 2, 6, 9, 15, 1, 7, 8)
PLANE_ORDER = (10, 9, 11, 6, 14, 2, 8, 5, 7, 13, 15, 1, 3, 4, 12)


def iota(shape, dim):
    return lax.broadcasted_iota(jnp.int32, shape, dim)


def split3(x):
    first = x.astype(BF16)
    rest = x - first.astype(F32)
    second = rest.astype(BF16)
    third = (rest - second.astype(F32)).astype(BF16)
    return first, second, third


def dot(a, b, dims=((1,), (0,)), precision=None):
    return lax.dot_general(a, b, (dims, ((), ())), precision=precision, preferred_element_type=F32)


def fused(
    hidden_ref, weight_ref, bias_hbm, seq_hbm, mask_hbm, labels_hbm,
    loss_hbm, wgrad_hbm, hgrad_hbm,
    loss_ref, hgrad_ref, bias_ref, seq_ref, mask_ref, labels_ref, wgrad_ref,
    hid, tags_ref, w, wsib, logit, fac, excess, mt, lg, lgp, lgs,
    pooled_six, sum_scale, ara, arb, pre, part, fars_in, fromm, fromp, acc, rtwo, zsend, zrecv,
    loc_sem, g_send, g_recv, h_send, h_recv, t_send, t_recv, e_send, e_recv, a_send, a_recv, b_send, b_recv,
    r_send, r_recv, s_send, s_recv, z_send, z_recv,
):
    width = hidden_ref.shape[1]
    half = width // 2
    voc = weight_ref.shape[1]
    d, v = lax.axis_index("dp"), lax.axis_index("vocab")
    core, y, xh = d % 2, (d // 2) % 4, d // 8
    xl, z = v % 2, v // 2
    x = xh * 2 + xl

    def place(px, py, pc, pz):
        return ((px // 2) * 8 + py * 2 + pc, pz * 2 + px % 2)

    def column_mate(k):
        return place(x, y, (core + k // DEPTH) % 2, (z + k % DEPTH) % DEPTH)

    def plane_mate(k):
        return place((x + k // SIDE) % SIDE, (y + k % SIDE) % SIDE, core, z)

    def remote(src, dst, send, recv, device):
        return pltpu.make_async_remote_copy(
            src_ref=src, dst_ref=dst, send_sem=send, recv_sem=recv, device_id=device, device_id_type=MESH
        )

    def all_sent(source, sem):
        remote(source, source, sem, sem, to_sib).wait_send()

    def all_here(target, sem):
        remote(target, target, sem, sem, to_sib).wait_recv()

    to_sib = place(x, y, 1 - core, z)

    w_copies = [
        pltpu.make_async_copy(weight_ref.at[pl.ds(h * half, half), :], w.at[h], loc_sem.at[h]) for h in range(2)
    ]
    quad = width // 4
    seat_t = xh * 4 + y
    h_copies = [
        pltpu.make_async_copy(hidden_ref.at[:, pl.ds(q * quad, quad)], hid.at[core, seat_t, q], loc_sem.at[2 + q])
        for q in range(4)
    ]
    small_copies = [
        pltpu.make_async_copy(src, dst, loc_sem.at[6 + i])
        for i, (src, dst) in enumerate(
            ((seq_hbm, seq_ref), (mask_hbm, mask_ref), (bias_hbm, bias_ref), (labels_hbm, labels_ref))
        )
    ]
    for copy in small_copies[:2] + h_copies + w_copies + small_copies[2:]:
        copy.start()

    barrier = pltpu.get_barrier_semaphore()
    for k in (2, 1, 3):
        pl.semaphore_signal(barrier, inc=1, device_id=plane_mate(k), device_id_type=MESH)
    for k in (1, 7, 8):
        pl.semaphore_signal(barrier, inc=1, device_id=column_mate(k), device_id_type=MESH)
    for k in range(4, PAIR):
        pl.semaphore_signal(barrier, inc=1, device_id=plane_mate(k), device_id_type=MESH)
    for k in (2, 3, 4, 5, 6, 9, 10, 11, 12, 13, 14, 15):
        pl.semaphore_signal(barrier, inc=1, device_id=column_mate(k), device_id_type=MESH)

    eye = iota((TOK, TOK), 0) == iota((TOK, TOK), 1)
    for copy in small_copies[:2]:
        copy.wait()
    tag_row = jnp.where(mask_ref[...] > 0, seq_ref[...], SEQ_GROUP).astype(F32)
    tag_col = jnp.sum(jnp.where(eye, jnp.broadcast_to(tag_row, (TOK, TOK)), 0.0), axis=1, keepdims=True)
    tags_ref[core, seat_t] = jnp.broadcast_to(tag_col, (TOK, TAG)).astype(BF16)
    pl.semaphore_wait(barrier, 2 * (PAIR - 1))

    up, down, far = (y + 1) % 4, (y + 3) % 4, (y + 2) % 4
    other = 1 - xh
    cross_x = other * 2 + 1 - xl
    colour = (z + 2 * xl) % 4
    to_twin = place(xh * 2 + 1 - xl, y, core, z)
    to_above = place(x, y, core, (z + 1) % DEPTH)
    to_below = place(x, y, core, (z + DEPTH - 1) % DEPTH)

    def spot(n, rq, of_core=core):
        row = (xh if n < 4 else other) * 4 + (y, up, down, far)[n % 4]
        return hid.at[of_core, row, (colour + rq) % 4]

    fetches = (
        (place(cross_x, y, core, z), 4, 2, (0, 1, 3)),
        (place(x, down, core, z), 1, 0, (0, 2, 1)),
        (place(x, up, core, z), 2, 0, (0, 2, 3)),
        (place(x, far, core, z), 3, 0, (0,)),
        (place(cross_x, down, core, z), 5, 2, (0,)),
        (place(cross_x, up, core, z), 6, 2, (0,)),
        (place(cross_x, far, core, z), 7, 2, (0,)),
    )
    def post(chunks, levels):
        for level in levels:
            for device, n, shift, quarters in fetches:
                if n in chunks and level < len(quarters):
                    rq = quarters[level]
                    q = (colour + shift + rq) % 4
                    src = hid.at[core, seat_t, q]
                    remote(src, src, g_send, g_recv.at[n * 4 + rq], device).start()

    for copy in h_copies:
        copy.wait()
    post((1, 2, 3, 4, 5, 6, 7), (0,))
    own_tags = tags_ref.at[core, seat_t]
    for device, n, _, _ in fetches:
        remote(own_tags, own_tags, t_send.at[0], t_recv.at[n], device).start()

    def hand_over(n, rq):
        chunk = spot(n, rq)
        remote(chunk, chunk, h_send, h_recv.at[n], to_sib).start()

    def arrived(n, rq):
        chunk = spot(n, rq)
        all_here(chunk, g_recv.at[n * 4 + rq])

    for rq in range(4):
        hand_over(0, rq)
    for copy in w_copies + small_copies[2:]:
        copy.wait()
    w_swap = remote(w.at[1 - core], wsib, e_send.at[0], e_recv.at[0], to_sib)
    w_swap.start()

    for n in (4, 1, 2, 3, 5, 6, 7):
        arrived(n, 0)
        chunk = spot(n, 0)
        for device, rq, skipped in ((to_twin, 2, (1, 2)), (to_above, 3, (2, 4)), (to_below, 1, (1, 4))):
            if n not in skipped:
                remote(chunk, chunk, g_send, g_recv.at[n * 4 + rq], device).start()
        if n == 4:
            post((1, 2, 4), (1,))
        if n == 3:
            post((1, 2, 4), (2,))
        hand_over(n, 0)
    for n in range(1, 8):
        there = tags_ref.at[core, (xh if n < 4 else other) * 4 + (y, up, down, far)[n % 4]]
        all_here(there, t_recv.at[n])
    remote(tags_ref.at[core], tags_ref.at[core], t_send.at[1], t_recv.at[0], to_sib).start()
    tokens = GROUPS * TOK
    deep = min(512, quad)
    per_half = half // deep
    per_quad = quad // deep
    share = tokens // 2

    def logits_of(c):
        rows = pl.ds(pl.multiple_of(c * share, share), share)
        bias = jnp.concatenate([bias_ref[b : b + 1, :] for b in range(voc // TAG)], axis=1)
        value = jnp.broadcast_to(bias, (share, voc))
        for q in range(4):
            a = hid[c, :, q].reshape(share, quad)
            value = value + dot(a, w[q // 2, pl.ds((q % 2) * quad, quad), :])
        logit[rows, :] = value

        def excess_step(i, carry):
            rows = pl.ds(pl.multiple_of(c * share + i * 64, 64), 64)
            l = logit[rows, :]
            soft = jnp.maximum(l, 0.0) + jnp.log1p(jnp.exp(-jnp.abs(l)))
            u = 1.0 + jnp.log1p(soft)
            u2 = u * u
            excess[rows, :] = u2 * u2 - 1.0
            return carry

        lax.fori_loop(0, 4, excess_step, 0)

    def complete(chunks):
        for n in chunks:
            for rq in (2, 3, 1):
                arrived(n, rq)
                hand_over(n, rq)

    def handed(chunks):
        for n in chunks:
            row = (xh if n < 4 else other) * 4 + (y, up, down, far)[n % 4]
            all_here(hid.at[1 - core, row], h_recv.at[n])

    complete((1, 2, 3, 4, 5, 6, 7))
    logits_of(core)
    handed((0, 1, 2, 3, 4, 5, 6, 7))
    logits_of(1 - core)
    all_here(tags_ref.at[1 - core], t_recv.at[0])

    tags = tags_ref[...].reshape(tokens, TAG).astype(F32)
    row = iota((tokens, TAG), 0)
    lane = iota((tokens, TAG), 1)
    index = lane % 32
    wanted_group = index // 2
    wanted_tag = index % 2 + 2 * (lane // 32)
    belongs = (
        (2 * ((row % share) // TOK) + row // share == wanted_group)
        & (tags == wanted_tag.astype(F32))
        & (tags < SEQ_GROUP)
        & (lane < 64)
    )
    member_t = jnp.where(belongs, 1.0, 0.0)
    for i in range(3):
        mt[:, pl.ds(i * TAG, TAG)] = member_t.astype(BF16)
    member = jnp.transpose(member_t)
    inv_count = 1.0 / jnp.maximum(jnp.sum(member, axis=1, keepdims=True), 1.0)
    member = member.astype(BF16)

    e1, e2, e3 = split3(excess[...])
    pooled_sum = (dot(member, e1) + dot(member, e2) + dot(member, e3)) * inv_count
    pooled = jnp.log1p(pooled_sum) * 0.25
    p1, p2, p3 = split3(pooled)
    for i, piece in enumerate((p1, p2, p1, p3, p2, p1)):
        pooled_six[pl.ds(i * TAG, TAG), :] = piece
    sum_scale[...] = inv_count / (4.0 * (1.0 + pooled_sum))

    wide = iota((32, TAG), 1)
    in_passages = (wide >= 32) & (wide < 64)
    inner = dot(pooled[:32], pooled, ((1,), (1,)), precise)
    inner = jnp.where(in_passages, inner, 0.0)
    packed = inner[0:8]
    packed = pltpu.roll(packed, 96, 1)
    for b in range(1, 4):
        shift = 32 * (b - 1)
        piece = inner[8 * b : 8 * b + 8]
        packed = packed + (pltpu.roll(piece, shift, 1) if shift else piece)
    squares = dot(jnp.ones((8, voc), F32), pooled * pooled, ((1,), (1,)), precise)

    slot = core * DEPTH + z
    ara[slot, 0:8, :] = packed
    ara[slot, 8:9, :] = squares[0:1]
    message = pl.ds(0, 9)
    mail = ara.at[slot, message]
    for k in COLUMN_ORDER:
        remote(mail, mail, a_send, a_recv, column_mate(k)).start()

    def factor_step(i, carry):
        rows = pl.ds(pl.multiple_of(i * 64, 64), 64)
        l = logit[rows, :]
        e = jnp.exp(-jnp.abs(l))
        soft = jnp.maximum(l, 0.0) + jnp.log1p(e)
        u = 1.0 + jnp.log1p(soft)
        top = jnp.where(l >= 0.0, 1.0, e)
        fac[rows, :] = 4.0 * (u * u * u) * top / ((1.0 + e) * (1.0 + soft))
        return carry

    lax.fori_loop(0, GROUPS // 2, factor_step, 0)

    all_here(ara.at[pl.ds(1, PAIR - 1), message], a_recv)
    column_sum = ara[0, message]
    for k in range(1, PAIR):
        column_sum = column_sum + ara[k, message]
    slot_b = x * SIDE + y
    arb[slot_b, message] = column_sum
    mail = arb.at[slot_b, message]
    for k in PLANE_ORDER:
        remote(mail, mail, b_send, b_recv, plane_mate(k)).start()
    all_sent(hid.at[0, pl.ds(0, 7)], g_send)
    all_sent(hid.at[0], h_send)
    all_sent(tags_ref.at[0, pl.ds(0, 7)], t_send.at[0])
    all_sent(tags_ref.at[0], t_send.at[1])
    all_sent(ara.at[pl.ds(1, PAIR - 1), message], a_send)
    all_here(arb.at[pl.ds(1, PAIR - 1), message], b_recv)
    total = arb[0, message]
    for k in range(1, PAIR):
        total = total + arb[k, message]

    pieces = []
    for b in range(4):
        shift = (32 - 32 * b) % 128
        pieces.append(pltpu.roll(total[0:8], shift, 1) if shift else total[0:8])
    inner = jnp.where(in_passages, jnp.concatenate(pieces, axis=0), 0.0)
    square_row = total[8:9]
    eye_wide = iota((TAG, TAG), 0) == iota((TAG, TAG), 1)
    square_col = jnp.sum(jnp.where(eye_wide, jnp.broadcast_to(square_row, (TAG, TAG)), 0.0), axis=1, keepdims=True)
    norm_row = jnp.sqrt(square_row + norm_eps)
    norm_col = jnp.sqrt(square_col + norm_eps)
    cosine = inner / (norm_col[:32] * norm_row)
    scores = score_scale * cosine
    exp_scores = jnp.where(in_passages, jnp.exp(scores), 0.0)
    totals = jnp.sum(exp_scores, axis=0, keepdims=True)
    totals = jnp.where(in_passages[0:1], totals, 1.0)
    labels = labels_ref[...].astype(F32)
    label_col = jnp.sum(jnp.where(eye, jnp.broadcast_to(labels, (32, 32)), 0.0), axis=1, keepdims=True)
    row_id = iota((32, TAG), 0)
    label_row = jnp.sum(
        jnp.where(wide - 32 == row_id, jnp.broadcast_to(label_col, (32, TAG)), 0.0), axis=0, keepdims=True
    )
    chosen = jnp.where((row_id.astype(F32) == label_row) & in_passages, 1.0, 0.0)
    per_passage = jnp.log(totals) - jnp.sum(chosen * scores, axis=0, keepdims=True)
    score_grad = (loss_scale * score_scale / 32.0) * (exp_scores / totals - chosen)
    blank = jnp.zeros((TAG - 32, TAG), F32)
    grad_full = jnp.concatenate([score_grad, blank], axis=0)
    cos_full = jnp.concatenate([cosine, blank], axis=0)
    grad_sym = grad_full + jnp.transpose(grad_full)
    cos_sym = cos_full + jnp.transpose(cos_full)
    radial = jnp.sum(grad_sym * cos_sym, axis=1, keepdims=True)
    inv_col, inv_row = 1.0 / norm_col, 1.0 / norm_row
    mix = inv_col * (grad_sym * inv_row - jnp.where(eye_wide, radial * inv_col, 0.0))
    m1, m2, m3 = split3(mix)
    sum_grad = dot(jnp.concatenate([m1, m1, m2, m1, m2, m3], axis=1), pooled_six[...]) * sum_scale[...]

    thirds = jnp.concatenate(split3(sum_grad), axis=0)
    new, old = iota((128, 128), 0), iota((128, 128), 1)
    source = (new // 32) * 32 + ((new // 2) % 8) * 4 + ((new // 16) % 2) * 2 + new % 2
    shuffle = jnp.where(source == old, 1.0, 0.0).astype(BF16)
    lg_swaps = []
    for i in range(4):
        rows = pl.ds(i * 128, 128)
        g = (dot(mt[rows, :], thirds) * fac[rows, :]).astype(BF16)
        lg[rows, :] = g
        p = dot(shuffle, g).astype(BF16)
        cx, part_of = i % 2, pl.ds((i // 2) * 16, 16)
        for b in range(8):
            lgp[cx * 2 + b % 2, b // 2, part_of] = p[b * 16 : b * 16 + 16]
        box = (pl.ds(cx * 2, 2), slice(None), part_of)
        swap = remote(lgp.at[box], lgs.at[box], e_send.at[1 + i], e_recv.at[1 + i], to_sib)
        swap.start()
        lg_swaps.append(swap)

    loss_ref[...] = jnp.sum(per_passage, axis=1, keepdims=True) / 32.0

    span = half // 2
    side = span // 2

    def ring(o):
        return place((x + (1 - core) * o) % 4, (y + core * o) % 4, core, z)

    def ring_two(o):
        return place((x + core * o) % 4, (y + (1 - core) * o) % 4, core, z)

    def rows_of(ref, o):
        picked = []
        for i in range(4):
            px = (1 - core) * ((x + o) % 4) + core * i
            py = core * ((y + o) % 4) + (1 - core) * i
            picked.append(ref[px, py])
        return jnp.concatenate(picked, axis=0)

    def columns(n):
        return pl.ds(n * side, side)

    def term(rows, weights):
        return dot(rows, weights, ((1,), (1,)))

    def keep(o, n, value):
        part[o, :, :, columns(n)] = value.astype(BF16).reshape(4, 32, side)

    def partial(o, n, mine, theirs):
        keep(o, n, term(mine, w[core, columns(n), :]) + term(theirs, wsib[columns(n), :]))

    plus, minus = ring(1), ring(3)
    mine = rows_of(lgp, 2)
    for n in range(4):
        pre[:, columns(n)] = term(mine, w[core, columns(n), :])
    w_swap.wait_recv()
    for swap in lg_swaps:
        swap.wait_recv()
    theirs = rows_of(lgs, 2)
    fars = []
    for n in range(4):
        keep(2, n, pre[:, columns(n)] + term(theirs, wsib[columns(n), :]))
        copy = remote(part.at[2, :, :, columns(n)], fars_in.at[n], r_send, r_recv.at[n], (plus, minus)[n % 2])
        copy.start()
        fars.append(copy)
    mine_up, theirs_up = rows_of(lgp, 1), rows_of(lgs, 1)
    mine_down, theirs_down = rows_of(lgp, 3), rows_of(lgs, 3)
    firsts = []

    def pass_on(o, n, k):
        target, landing = ((plus, fromm) if o == 1 else (minus, fromp))
        copy = remote(part.at[o, :, :, columns(n)], landing.at[n], r_send, r_recv.at[k], target)
        copy.start()
        firsts.append(copy)

    for h in range(2):
        left, right = 2 * h, 2 * h + 1
        partial(1, right, mine_up, theirs_up)
        pass_on(1, right, 4 + right)
        partial(3, left, mine_down, theirs_down)
        pass_on(3, left, 4 + left)
        partial(1, left, mine_up, theirs_up)
        partial(3, right, mine_down, theirs_down)
        for n, o in ((left, 1), (right, 3)):
            fars[n].wait_recv()
            value = part[o, :, :, columns(n)].astype(F32) + fars_in[n].astype(F32)
            part[o, :, :, columns(n)] = value.astype(BF16)
            pass_on(o, n, 8 + n)
    mine, theirs = rows_of(lgp, 0), rows_of(lgs, 0)
    for n in range(4):
        partial(0, n, mine, theirs)

    def weight_step(i, carry):
        start = pl.multiple_of((i % per_quad) * deep, deep)
        a = hid[:, :, i // per_quad, :, pl.ds(start, deep)].reshape(tokens, deep)
        wgrad_ref[pl.ds(pl.multiple_of(i * deep, deep), deep), :] = dot(a, lg[...], ((0,), (0,))).astype(BF16)
        return carry

    seat = core * x + (1 - core) * y
    for h in range(2):
        lax.fori_loop(h * per_half, (h + 1) * per_half, weight_step, 0)
        for copy in firsts[4 * h : 4 * h + 4]:
            copy.wait_recv()
        for o in (2, 1, 3, 0):
            i = (seat + o) % 4
            for n in (2 * h, 2 * h + 1):
                cols = columns(n)
                value = part[0, i, :, cols].astype(F32) + fromm[n, i].astype(F32) + fromp[n, i].astype(F32)
                acc[h, i, :, pl.ds((n % 2) * side, side)] = value.astype(BF16)
            if o:
                k = h * 3 + o - 1
                copy = remote(acc.at[h, i], rtwo.at[k], s_send, s_recv.at[h], ring_two(o))
                copy.start()
    wg_copy = pltpu.make_async_copy(wgrad_ref, wgrad_hbm, loc_sem.at[10])
    wg_copy.start()
    w_swap.wait_send()
    for swap in lg_swaps:
        swap.wait_send()
    all_sent(arb.at[pl.ds(1, PAIR - 1), message], b_send)
    all_sent(part.at[pl.ds(0, 3)], r_send)

    slab = span // 8
    new, old = iota((256, 256), 0), iota((256, 256), 1)
    source = (new % 8) * 32 + (new // 16) * 2 + (new // 8) % 2
    shuffle = jnp.where(source == old, 1.0, 0.0).astype(BF16)
    for h in range(2):
        all_here(rtwo.at[pl.ds(3 * h, 3)], s_recv.at[h])
        rows = acc[h, seat].astype(F32)
        for o in range(3):
            rows = rows + rtwo[h * 3 + o].astype(F32)
        rows = rows.astype(BF16)
        stacked = jnp.concatenate([rows[:, b * slab : (b + 1) * slab] for b in range(8)], axis=0)
        zsend[h] = dot(shuffle, stacked).astype(BF16).reshape(16, 16, slab)
        for k in COLUMN_ORDER:
            target = ((core + k // DEPTH) % 2) * DEPTH + (z + k % DEPTH) % DEPTH
            remote(zsend.at[h, target], zrecv.at[h, slot], z_send, z_recv.at[h], column_mate(k)).start()
        zrecv[h, slot] = zsend[h, slot]
    all_sent(rtwo, s_send)
    for h in range(2):
        all_here(zrecv.at[h, pl.ds(1, PAIR - 1)], z_recv.at[h])
        for c in range(2):
            value = zrecv[h, c * DEPTH].astype(F32)
            for k in range(1, DEPTH):
                value = value + zrecv[h, c * DEPTH + k].astype(F32)
            for r in range(2):
                for b in range(8):
                    cols = pl.ds(c * half + h * span + b * slab, slab)
                    hgrad_ref[r : r + 1, cols] = value[r * 8 + b : r * 8 + b + 1]

    out_copies = [
        pltpu.make_async_copy(hgrad_ref, hgrad_hbm, loc_sem.at[11]),
        pltpu.make_async_copy(loss_ref, loss_hbm, loc_sem.at[12]),
    ]
    for copy in out_copies:
        copy.start()
    for h in range(2):
        all_sent(zsend.at[h, pl.ds(1, PAIR - 1)], z_send)
    for copy in out_copies:
        copy.wait()
    wg_copy.wait()


def finish(loss_in, wgrad_in, hgrad_in, loss_out, wgrad_out, hgrad_out, loss, wgrad, hgrad, load_sem, store_sem):
    step = wgrad.shape[0] // CHUNKS
    stages = [(hgrad_in, hgrad, hgrad_out), (loss_in, loss, loss_out)]
    for i in range(CHUNKS):
        rows = pl.ds(i * step, step)
        stages.append((wgrad_in.at[rows, :], wgrad.at[rows, :], wgrad_out.at[rows, :]))
    loads = [pltpu.make_async_copy(src, via, load_sem.at[i]) for i, (src, via, _) in enumerate(stages)]
    stores = [pltpu.make_async_copy(via, dst, store_sem.at[i]) for i, (_, via, dst) in enumerate(stages)]
    for copy in loads:
        copy.start()
    for load, store in zip(loads, stores):
        load.wait()
        store.start()
    for copy in stores:
        copy.wait()


def body(hidden, head_weight, vocab_bias, seq_ids, token_mask, labels):
    width, voc = head_weight.shape
    half = width // 2
    tokens = GROUPS * TOK
    hbm = pl.BlockSpec(memory_space=pltpu.HBM)
    dma = pltpu.SemaphoreType.DMA
    shapes = (
        jax.ShapeDtypeStruct((1, 1), F32),
        jax.ShapeDtypeStruct((width, voc), BF16),
        jax.ShapeDtypeStruct((2, width), F32),
    )
    results = pl.pallas_call(
        fused,
        out_shape=shapes,
        in_specs=[hbm] * 6,
        out_specs=(hbm, hbm, hbm),
        scratch_shapes=[
            pltpu.VMEM((1, 1), F32),
            pltpu.VMEM((2, width), F32),
            pltpu.VMEM((voc // TAG, TAG), F32),
            pltpu.VMEM((1, TOK), jnp.int32),
            pltpu.VMEM((1, TOK), jnp.int32),
            pltpu.VMEM((1, 32), jnp.int32),
            pltpu.VMEM((width, voc), BF16),
            pltpu.VMEM((2, GROUPS // 2, 4, TOK, width // 4), BF16),
            pltpu.VMEM((2, GROUPS // 2, TOK, TAG), BF16),
            pltpu.VMEM((2, half, voc), BF16),
            pltpu.VMEM((half, voc), BF16),
            pltpu.VMEM((tokens, voc), F32),
            pltpu.VMEM((tokens, voc), F32),
            pltpu.VMEM((tokens, voc), F32),
            pltpu.VMEM((tokens, 3 * TAG), BF16),
            pltpu.VMEM((tokens, voc), BF16),
            pltpu.VMEM((4, 4, TOK, voc), BF16),
            pltpu.VMEM((4, 4, TOK, voc), BF16),
            pltpu.VMEM((6 * TAG, voc), BF16),
            pltpu.VMEM((TAG, voc), F32),
            pltpu.VMEM((PAIR, 16, TAG), F32),
            pltpu.VMEM((PAIR, 16, TAG), F32),
            pltpu.VMEM((4 * TOK, half), F32),
            pltpu.VMEM((4, 4, TOK, half), BF16),
            pltpu.VMEM((4, 4, TOK, half // 4), BF16),
            pltpu.VMEM((4, 4, TOK, half // 4), BF16),
            pltpu.VMEM((4, 4, TOK, half // 4), BF16),
            pltpu.VMEM((2, 4, TOK, half // 2), BF16),
            pltpu.VMEM((6, TOK, half // 2), BF16),
            pltpu.VMEM((2, PAIR, 16, half // 16), BF16),
            pltpu.VMEM((2, PAIR, 16, half // 16), BF16),
            dma((13,)),
            dma,
            dma((32,)),
            dma,
            dma((8,)),
            dma((2,)),
            dma((8,)),
            dma((5,)),
            dma((5,)),
            dma,
            dma,
            dma,
            dma,
            dma,
            dma((12,)),
            dma,
            dma((2,)),
            dma,
            dma((2,)),
        ],
        compiler_params=pltpu.CompilerParams(
            collective_id=0, has_side_effects=True, vmem_limit_bytes=60 * 1024 * 1024
        ),
        name="splade_head",
    )(
        hidden,
        head_weight,
        vocab_bias.reshape(voc // TAG, TAG),
        seq_ids,
        token_mask,
        labels.reshape(1, labels.shape[0]),
    )
    loss, weight_grad, hidden_grad = pl.pallas_call(
        finish,
        out_shape=shapes,
        in_specs=[hbm] * 3,
        out_specs=(hbm,) * 3,
        scratch_shapes=[
            *(pltpu.VMEM(shape.shape, shape.dtype) for shape in shapes),
            dma((CHUNKS + 2,)),
            dma((CHUNKS + 2,)),
        ],
        compiler_params=pltpu.CompilerParams(vmem_limit_bytes=60 * 1024 * 1024),
        name="results",
    )(*results)
    return loss.reshape(()), weight_grad, hidden_grad


def solution(mesh):
    in_specs = (
        P("dp", None),
        P(None, ("dp", "vocab")),
        P(("dp", "vocab")),
        P("dp", None),
        P("dp", None),
        P(),
    )
    out_specs = (P(), P(None, ("dp", "vocab")), P(("dp", "vocab"), None))
    return jax.shard_map(body, mesh=mesh, in_specs=in_specs, out_specs=out_specs, check_vma=False)
```

```python
import functools

import jax
import jax.numpy as jnp
from jax import lax
from jax.experimental import pallas as pl
from jax.experimental.pallas import tpu as pltpu
from jax.sharding import PartitionSpec as P

MESH = pl.DeviceIdType.MESH
F32, BF16 = jnp.float32, jnp.bfloat16

SEQ_GROUP = 4
GROUPS = 16
TOK = 32
SIDE = 4
DEPTH = 8
TAG = 128

score_scale = 20.0
loss_scale = 65536.0
norm_eps = 1e-06
precise = lax.Precision.HIGHEST

PAIR = 16
CHUNKS = 8
COLUMN_ORDER = (12, 4, 11, 13, 3, 5, 10, 14, 2, 6, 9, 15, 1, 7, 8)
PLANE_ORDER = (10, 9, 11, 6, 14, 2, 8, 5, 7, 13, 15, 1, 3, 4, 12)


def iota(shape, dim):
    return lax.broadcasted_iota(jnp.int32, shape, dim)


def split3(x):
    first = x.astype(BF16)
    rest = x - first.astype(F32)
    second = rest.astype(BF16)
    third = (rest - second.astype(F32)).astype(BF16)
    return first, second, third


def dot(a, b, dims=((1,), (0,)), precision=None):
    return lax.dot_general(a, b, (dims, ((), ())), precision=precision, preferred_element_type=F32)


def fused(
    hidden_ref, weight_ref, bias_hbm, seq_hbm, mask_hbm, labels_hbm,
    loss_hbm, wgrad_hbm, hgrad_hbm,
    loss_ref, hgrad_ref, bias_ref, seq_ref, mask_ref, labels_ref, wgrad_ref,
    hid, tags_ref, w, wsib, logit, fac, excess, mt, lg, lgp, lgs,
    pooled_six, sum_scale, ara, arb, pre, part, fars_in, fromm, fromp, acc, rtwo, zsend, zrecv,
    loc_sem, g_send, g_recv, h_send, h_recv, t_send, t_recv, e_send, e_recv, a_send, a_recv, b_send, b_recv,
    r_send, r_recv, s_send, s_recv, z_send, z_recv,
):
    width = hidden_ref.shape[1]
    half = width // 2
    voc = weight_ref.shape[1]
    d, v = lax.axis_index("dp"), lax.axis_index("vocab")
    core, y, xh = d % 2, (d // 2) % 4, d // 8
    xl, z = v % 2, v // 2
    x = xh * 2 + xl

    def place(px, py, pc, pz):
        return ((px // 2) * 8 + py * 2 + pc, pz * 2 + px % 2)

    def column_mate(k):
        return place(x, y, (core + k // DEPTH) % 2, (z + k % DEPTH) % DEPTH)

    def plane_mate(k):
        return place((x + k // SIDE) % SIDE, (y + k % SIDE) % SIDE, core, z)

    def remote(src, dst, send, recv, device):
        return pltpu.make_async_remote_copy(
            src_ref=src, dst_ref=dst, send_sem=send, recv_sem=recv, device_id=device, device_id_type=MESH
        )

    def all_sent(source, sem):
        remote(source, source, sem, sem, to_sib).wait_send()

    def all_here(target, sem):
        remote(target, target, sem, sem, to_sib).wait_recv()

    to_sib = place(x, y, 1 - core, z)

    w_copies = [
        pltpu.make_async_copy(weight_ref.at[pl.ds(h * half, half), :], w.at[h], loc_sem.at[h]) for h in range(2)
    ]
    quad = width // 4
    seat_t = xh * 4 + y
    h_copies = [
        pltpu.make_async_copy(hidden_ref.at[:, pl.ds(q * quad, quad)], hid.at[core, seat_t, q], loc_sem.at[2 + q])
        for q in range(4)
    ]
    small_copies = [
        pltpu.make_async_copy(src, dst, loc_sem.at[6 + i])
        for i, (src, dst) in enumerate(
            ((seq_hbm, seq_ref), (mask_hbm, mask_ref), (bias_hbm, bias_ref), (labels_hbm, labels_ref))
        )
    ]
    for copy in small_copies[:2] + h_copies + w_copies + small_copies[2:]:
        copy.start()

    barrier = pltpu.get_barrier_semaphore()
    for k in (2, 1, 3):
        pl.semaphore_signal(barrier, inc=1, device_id=plane_mate(k), device_id_type=MESH)
    for k in (1, 7, 8):
        pl.semaphore_signal(barrier, inc=1, device_id=column_mate(k), device_id_type=MESH)
    for k in range(4, PAIR):
        pl.semaphore_signal(barrier, inc=1, device_id=plane_mate(k), device_id_type=MESH)
    for k in (2, 3, 4, 5, 6, 9, 10, 11, 12, 13, 14, 15):
        pl.semaphore_signal(barrier, inc=1, device_id=column_mate(k), device_id_type=MESH)

    eye = iota((TOK, TOK), 0) == iota((TOK, TOK), 1)
    for copy in small_copies[:2]:
        copy.wait()
    tag_row = jnp.where(mask_ref[...] > 0, seq_ref[...], SEQ_GROUP).astype(F32)
    tag_col = jnp.sum(jnp.where(eye, jnp.broadcast_to(tag_row, (TOK, TOK)), 0.0), axis=1, keepdims=True)
    tags_ref[core, seat_t] = jnp.broadcast_to(tag_col, (TOK, TAG)).astype(BF16)
    pl.semaphore_wait(barrier, 2 * (PAIR - 1))

    up, down, far = (y + 1) % 4, (y + 3) % 4, (y + 2) % 4
    other = 1 - xh
    cross_x = other * 2 + 1 - xl
    colour = (z + 2 * xl) % 4
    to_twin = place(xh * 2 + 1 - xl, y, core, z)
    to_above = place(x, y, core, (z + 1) % DEPTH)
    to_below = place(x, y, core, (z + DEPTH - 1) % DEPTH)

    def spot(n, rq, of_core=core):
        row = (xh if n < 4 else other) * 4 + (y, up, down, far)[n % 4]
        return hid.at[of_core, row, (colour + rq) % 4]

    fetches = (
        (place(cross_x, y, core, z), 4, 2, (0, 1, 3)),
        (place(x, down, core, z), 1, 0, (0, 2, 1)),
        (place(x, up, core, z), 2, 0, (0, 2, 3)),
        (place(x, far, core, z), 3, 0, (0,)),
        (place(cross_x, down, core, z), 5, 2, (0,)),
        (place(cross_x, up, core, z), 6, 2, (0,)),
        (place(cross_x, far, core, z), 7, 2, (0,)),
    )
    def post(chunks, levels):
        for level in levels:
            for device, n, shift, quarters in fetches:
                if n in chunks and level < len(quarters):
                    rq = quarters[level]
                    q = (colour + shift + rq) % 4
                    src = hid.at[core, seat_t, q]
                    remote(src, src, g_send, g_recv.at[n * 4 + rq], device).start()

    for copy in h_copies:
        copy.wait()
    post((1, 2, 3, 4, 5, 6, 7), (0,))
    own_tags = tags_ref.at[core, seat_t]
    for device, n, _, _ in fetches:
        remote(own_tags, own_tags, t_send.at[0], t_recv.at[n], device).start()

    def hand_over(n, rq):
        chunk = spot(n, rq)
        remote(chunk, chunk, h_send, h_recv.at[n], to_sib).start()

    def arrived(n, rq):
        chunk = spot(n, rq)
        all_here(chunk, g_recv.at[n * 4 + rq])

    for rq in range(4):
        hand_over(0, rq)
    for copy in w_copies + small_copies[2:]:
        copy.wait()
    w_swap = remote(w.at[1 - core], wsib, e_send.at[0], e_recv.at[0], to_sib)
    w_swap.start()

    for n in (4, 1, 2, 3, 5, 6, 7):
        arrived(n, 0)
        chunk = spot(n, 0)
        for device, rq, skipped in ((to_twin, 2, (1, 2)), (to_above, 3, (2, 4)), (to_below, 1, (1, 4))):
            if n not in skipped:
                remote(chunk, chunk, g_send, g_recv.at[n * 4 + rq], device).start()
        if n == 4:
            post((1, 2, 4), (1,))
        if n == 3:
            post((1, 2, 4), (2,))
        hand_over(n, 0)
    for n in range(1, 8):
        there = tags_ref.at[core, (xh if n < 4 else other) * 4 + (y, up, down, far)[n % 4]]
        all_here(there, t_recv.at[n])
    remote(tags_ref.at[core], tags_ref.at[core], t_send.at[1], t_recv.at[0], to_sib).start()
    tokens = GROUPS * TOK
    deep = min(512, quad)
    per_half = half // deep
    per_quad = quad // deep
    share = tokens // 2

    def logits_of(c):
        rows = pl.ds(pl.multiple_of(c * share, share), share)
        bias = jnp.concatenate([bias_ref[b : b + 1, :] for b in range(voc // TAG)], axis=1)
        value = jnp.broadcast_to(bias, (share, voc))
        for q in range(4):
            a = hid[c, :, q].reshape(share, quad)
            value = value + dot(a, w[q // 2, pl.ds((q % 2) * quad, quad), :])
        logit[rows, :] = value

        def excess_step(i, carry):
            rows = pl.ds(pl.multiple_of(c * share + i * 64, 64), 64)
            l = logit[rows, :]
            soft = jnp.maximum(l, 0.0) + jnp.log1p(jnp.exp(-jnp.abs(l)))
            u = 1.0 + jnp.log1p(soft)
            u2 = u * u
            excess[rows, :] = u2 * u2 - 1.0
            return carry

        lax.fori_loop(0, 4, excess_step, 0)

    def complete(chunks):
        for n in chunks:
            for rq in (2, 3, 1):
                arrived(n, rq)
                hand_over(n, rq)

    def handed(chunks):
        for n in chunks:
            row = (xh if n < 4 else other) * 4 + (y, up, down, far)[n % 4]
            all_here(hid.at[1 - core, row], h_recv.at[n])

    complete((1, 2, 3, 4, 5, 6, 7))
    logits_of(core)
    handed((0, 1, 2, 3, 4, 5, 6, 7))
    logits_of(1 - core)
    all_here(tags_ref.at[1 - core], t_recv.at[0])

    tags = tags_ref[...].reshape(tokens, TAG).astype(F32)
    row = iota((tokens, TAG), 0)
    lane = iota((tokens, TAG), 1)
    index = lane % 32
    wanted_group = index // 2
    wanted_tag = index % 2 + 2 * (lane // 32)
    belongs = (
        (2 * ((row % share) // TOK) + row // share == wanted_group)
        & (tags == wanted_tag.astype(F32))
        & (tags < SEQ_GROUP)
        & (lane < 64)
    )
    member_t = jnp.where(belongs, 1.0, 0.0)
    for i in range(3):
        mt[:, pl.ds(i * TAG, TAG)] = member_t.astype(BF16)
    member = jnp.transpose(member_t)
    inv_count = 1.0 / jnp.maximum(jnp.sum(member, axis=1, keepdims=True), 1.0)
    member = member.astype(BF16)

    e1, e2, e3 = split3(excess[...])
    pooled_sum = (dot(member, e1) + dot(member, e2) + dot(member, e3)) * inv_count
    pooled = jnp.log1p(pooled_sum) * 0.25
    p1, p2, p3 = split3(pooled)
    for i, piece in enumerate((p1, p2, p1, p3, p2, p1)):
        pooled_six[pl.ds(i * TAG, TAG), :] = piece
    sum_scale[...] = inv_count / (4.0 * (1.0 + pooled_sum))

    wide = iota((32, TAG), 1)
    in_passages = (wide >= 32) & (wide < 64)
    inner = dot(pooled[:32], pooled, ((1,), (1,)), precise)
    inner = jnp.where(in_passages, inner, 0.0)
    packed = inner[0:8]
    packed = pltpu.roll(packed, 96, 1)
    for b in range(1, 4):
        shift = 32 * (b - 1)
        piece = inner[8 * b : 8 * b + 8]
        packed = packed + (pltpu.roll(piece, shift, 1) if shift else piece)
    squares = dot(jnp.ones((8, voc), F32), pooled * pooled, ((1,), (1,)), precise)

    slot = core * DEPTH + z
    ara[slot, 0:8, :] = packed
    ara[slot, 8:9, :] = squares[0:1]
    message = pl.ds(0, 9)
    mail = ara.at[slot, message]
    for k in COLUMN_ORDER:
        remote(mail, mail, a_send, a_recv, column_mate(k)).start()

    def factor_step(i, carry):
        rows = pl.ds(pl.multiple_of(i * 64, 64), 64)
        l = logit[rows, :]
        e = jnp.exp(-jnp.abs(l))
        soft = jnp.maximum(l, 0.0) + jnp.log1p(e)
        u = 1.0 + jnp.log1p(soft)
        top = jnp.where(l >= 0.0, 1.0, e)
        fac[rows, :] = 4.0 * (u * u * u) * top / ((1.0 + e) * (1.0 + soft))
        return carry

    lax.fori_loop(0, GROUPS // 2, factor_step, 0)

    all_here(ara.at[pl.ds(1, PAIR - 1), message], a_recv)
    column_sum = ara[0, message]
    for k in range(1, PAIR):
        column_sum = column_sum + ara[k, message]
    slot_b = x * SIDE + y
    arb[slot_b, message] = column_sum
    mail = arb.at[slot_b, message]
    for k in PLANE_ORDER:
        remote(mail, mail, b_send, b_recv, plane_mate(k)).start()
    all_sent(hid.at[0, pl.ds(0, 7)], g_send)
    all_sent(hid.at[0], h_send)
    all_sent(tags_ref.at[0, pl.ds(0, 7)], t_send.at[0])
    all_sent(tags_ref.at[0], t_send.at[1])
    all_sent(ara.at[pl.ds(1, PAIR - 1), message], a_send)
    all_here(arb.at[pl.ds(1, PAIR - 1), message], b_recv)
    total = arb[0, message]
    for k in range(1, PAIR):
        total = total + arb[k, message]

    pieces = []
    for b in range(4):
        shift = (32 - 32 * b) % 128
        pieces.append(pltpu.roll(total[0:8], shift, 1) if shift else total[0:8])
    inner = jnp.where(in_passages, jnp.concatenate(pieces, axis=0), 0.0)
    square_row = total[8:9]
    eye_wide = iota((TAG, TAG), 0) == iota((TAG, TAG), 1)
    square_col = jnp.sum(jnp.where(eye_wide, jnp.broadcast_to(square_row, (TAG, TAG)), 0.0), axis=1, keepdims=True)
    norm_row = jnp.sqrt(square_row + norm_eps)
    norm_col = jnp.sqrt(square_col + norm_eps)
    cosine = inner / (norm_col[:32] * norm_row)
    scores = score_scale * cosine
    exp_scores = jnp.where(in_passages, jnp.exp(scores), 0.0)
    totals = jnp.sum(exp_scores, axis=0, keepdims=True)
    totals = jnp.where(in_passages[0:1], totals, 1.0)
    labels = labels_ref[...].astype(F32)
    label_col = jnp.sum(jnp.where(eye, jnp.broadcast_to(labels, (32, 32)), 0.0), axis=1, keepdims=True)
    row_id = iota((32, TAG), 0)
    label_row = jnp.sum(
        jnp.where(wide - 32 == row_id, jnp.broadcast_to(label_col, (32, TAG)), 0.0), axis=0, keepdims=True
    )
    chosen = jnp.where((row_id.astype(F32) == label_row) & in_passages, 1.0, 0.0)
    per_passage = jnp.log(totals) - jnp.sum(chosen * scores, axis=0, keepdims=True)
    score_grad = (loss_scale * score_scale / 32.0) * (exp_scores / totals - chosen)
    blank = jnp.zeros((TAG - 32, TAG), F32)
    grad_full = jnp.concatenate([score_grad, blank], axis=0)
    cos_full = jnp.concatenate([cosine, blank], axis=0)
    grad_sym = grad_full + jnp.transpose(grad_full)
    cos_sym = cos_full + jnp.transpose(cos_full)
    radial = jnp.sum(grad_sym * cos_sym, axis=1, keepdims=True)
    inv_col, inv_row = 1.0 / norm_col, 1.0 / norm_row
    mix = inv_col * (grad_sym * inv_row - jnp.where(eye_wide, radial * inv_col, 0.0))
    m1, m2, m3 = split3(mix)
    sum_grad = dot(jnp.concatenate([m1, m1, m2, m1, m2, m3], axis=1), pooled_six[...]) * sum_scale[...]

    thirds = jnp.concatenate(split3(sum_grad), axis=0)
    new, old = iota((128, 128), 0), iota((128, 128), 1)
    source = (new // 32) * 32 + ((new // 2) % 8) * 4 + ((new // 16) % 2) * 2 + new % 2
    shuffle = jnp.where(source == old, 1.0, 0.0).astype(BF16)
    lg_swaps = []
    for i in range(4):
        rows = pl.ds(i * 128, 128)
        g = (dot(mt[rows, :], thirds) * fac[rows, :]).astype(BF16)
        lg[rows, :] = g
        p = dot(shuffle, g).astype(BF16)
        cx, part_of = i % 2, pl.ds((i // 2) * 16, 16)
        for b in range(8):
            lgp[cx * 2 + b % 2, b // 2, part_of] = p[b * 16 : b * 16 + 16]
        box = (pl.ds(cx * 2, 2), slice(None), part_of)
        swap = remote(lgp.at[box], lgs.at[box], e_send.at[1 + i], e_recv.at[1 + i], to_sib)
        swap.start()
        lg_swaps.append(swap)

    loss_ref[...] = jnp.sum(per_passage, axis=1, keepdims=True) / 32.0

    span = half // 2
    side = span // 2

    def ring(o):
        return place((x + (1 - core) * o) % 4, (y + core * o) % 4, core, z)

    def ring_two(o):
        return place((x + core * o) % 4, (y + (1 - core) * o) % 4, core, z)

    def rows_of(ref, o):
        picked = []
        for i in range(4):
            px = (1 - core) * ((x + o) % 4) + core * i
            py = core * ((y + o) % 4) + (1 - core) * i
            picked.append(ref[px, py])
        return jnp.concatenate(picked, axis=0)

    def columns(n):
        return pl.ds(n * side, side)

    def term(rows, weights):
        return dot(rows, weights, ((1,), (1,)))

    def keep(o, n, value):
        part[o, :, :, columns(n)] = value.astype(BF16).reshape(4, 32, side)

    def partial(o, n, mine, theirs):
        weights = jnp.concatenate([w[core, columns(n), :], wsib[columns(n), :]], axis=1)
        keep(o, n, term(jnp.concatenate([mine, theirs], axis=1), weights))

    plus, minus = ring(1), ring(3)
    mine = rows_of(lgp, 2)
    for n in range(4):
        pre[:, columns(n)] = term(mine, w[core, columns(n), :])
    w_swap.wait_recv()
    for swap in lg_swaps:
        swap.wait_recv()
    theirs = rows_of(lgs, 2)
    fars = []
    for n in range(4):
        keep(2, n, pre[:, columns(n)] + term(theirs, wsib[columns(n), :]))
        copy = remote(part.at[2, :, :, columns(n)], fars_in.at[n], r_send, r_recv.at[n], (plus, minus)[n % 2])
        copy.start()
        fars.append(copy)
    mine_up, theirs_up = rows_of(lgp, 1), rows_of(lgs, 1)
    mine_down, theirs_down = rows_of(lgp, 3), rows_of(lgs, 3)
    firsts = []

    def pass_on(o, n, k):
        target, landing = ((plus, fromm) if o == 1 else (minus, fromp))
        copy = remote(part.at[o, :, :, columns(n)], landing.at[n], r_send, r_recv.at[k], target)
        copy.start()
        firsts.append(copy)

    for h in range(2):
        left, right = 2 * h, 2 * h + 1
        partial(1, right, mine_up, theirs_up)
        pass_on(1, right, 4 + right)
        partial(3, left, mine_down, theirs_down)
        pass_on(3, left, 4 + left)
        partial(1, left, mine_up, theirs_up)
        partial(3, right, mine_down, theirs_down)
        for n, o in ((left, 1), (right, 3)):
            fars[n].wait_recv()
            value = part[o, :, :, columns(n)].astype(F32) + fars_in[n].astype(F32)
            part[o, :, :, columns(n)] = value.astype(BF16)
            pass_on(o, n, 8 + n)
    mine, theirs = rows_of(lgp, 0), rows_of(lgs, 0)
    for n in range(4):
        partial(0, n, mine, theirs)

    def weight_step(i, carry):
        start = pl.multiple_of((i % per_quad) * deep, deep)
        a = hid[:, :, i // per_quad, :, pl.ds(start, deep)].reshape(tokens, deep)
        wgrad_ref[pl.ds(pl.multiple_of(i * deep, deep), deep), :] = dot(a, lg[...], ((0,), (0,))).astype(BF16)
        return carry

    seat = core * x + (1 - core) * y
    for h in range(2):
        lax.fori_loop(h * per_half, (h + 1) * per_half, weight_step, 0)
        for copy in firsts[4 * h : 4 * h + 4]:
            copy.wait_recv()
        for o in (2, 1, 3, 0):
            i = (seat + o) % 4
            for n in (2 * h, 2 * h + 1):
                cols = columns(n)
                value = part[0, i, :, cols].astype(F32) + fromm[n, i].astype(F32) + fromp[n, i].astype(F32)
                acc[h, i, :, pl.ds((n % 2) * side, side)] = value.astype(BF16)
            if o:
                k = h * 3 + o - 1
                copy = remote(acc.at[h, i], rtwo.at[k], s_send, s_recv.at[h], ring_two(o))
                copy.start()
    wg_copy = pltpu.make_async_copy(wgrad_ref, wgrad_hbm, loc_sem.at[10])
    wg_copy.start()
    w_swap.wait_send()
    for swap in lg_swaps:
        swap.wait_send()
    all_sent(arb.at[pl.ds(1, PAIR - 1), message], b_send)
    all_sent(part.at[pl.ds(0, 3)], r_send)

    slab = span // 8
    new, old = iota((256, 256), 0), iota((256, 256), 1)
    source = (new % 8) * 32 + (new // 16) * 2 + (new // 8) % 2
    shuffle = jnp.where(source == old, 1.0, 0.0).astype(BF16)
    for h in range(2):
        all_here(rtwo.at[pl.ds(3 * h, 3)], s_recv.at[h])
        rows = acc[h, seat].astype(F32)
        for o in range(3):
            rows = rows + rtwo[h * 3 + o].astype(F32)
        rows = rows.astype(BF16)
        stacked = jnp.concatenate([rows[:, b * slab : (b + 1) * slab] for b in range(8)], axis=0)
        zsend[h] = dot(shuffle, stacked).astype(BF16).reshape(16, 16, slab)
        for k in COLUMN_ORDER:
            target = ((core + k // DEPTH) % 2) * DEPTH + (z + k % DEPTH) % DEPTH
            remote(zsend.at[h, target], zrecv.at[h, slot], z_send, z_recv.at[h], column_mate(k)).start()
        zrecv[h, slot] = zsend[h, slot]
    all_sent(rtwo, s_send)
    for h in range(2):
        all_here(zrecv.at[h, pl.ds(1, PAIR - 1)], z_recv.at[h])
        for c in range(2):
            value = zrecv[h, c * DEPTH].astype(F32)
            for k in range(1, DEPTH):
                value = value + zrecv[h, c * DEPTH + k].astype(F32)
            for r in range(2):
                for b in range(8):
                    cols = pl.ds(c * half + h * span + b * slab, slab)
                    hgrad_ref[r : r + 1, cols] = value[r * 8 + b : r * 8 + b + 1]

    out_copies = [
        pltpu.make_async_copy(hgrad_ref, hgrad_hbm, loc_sem.at[11]),
        pltpu.make_async_copy(loss_ref, loss_hbm, loc_sem.at[12]),
    ]
    for copy in out_copies:
        copy.start()
    for h in range(2):
        all_sent(zsend.at[h, pl.ds(1, PAIR - 1)], z_send)
    for copy in out_copies:
        copy.wait()
    wg_copy.wait()


def finish(loss_in, wgrad_in, hgrad_in, loss_out, wgrad_out, hgrad_out, loss, wgrad, hgrad, load_sem, store_sem):
    step = wgrad.shape[0] // CHUNKS
    stages = [(hgrad_in, hgrad, hgrad_out), (loss_in, loss, loss_out)]
    for i in range(CHUNKS):
        rows = pl.ds(i * step, step)
        stages.append((wgrad_in.at[rows, :], wgrad.at[rows, :], wgrad_out.at[rows, :]))
    loads = [pltpu.make_async_copy(src, via, load_sem.at[i]) for i, (src, via, _) in enumerate(stages)]
    stores = [pltpu.make_async_copy(via, dst, store_sem.at[i]) for i, (_, via, dst) in enumerate(stages)]
    for copy in loads:
        copy.start()
    for load, store in zip(loads, stores):
        load.wait()
        store.start()
    for copy in stores:
        copy.wait()


def body(hidden, head_weight, vocab_bias, seq_ids, token_mask, labels):
    width, voc = head_weight.shape
    half = width // 2
    tokens = GROUPS * TOK
    hbm = pl.BlockSpec(memory_space=pltpu.HBM)
    dma = pltpu.SemaphoreType.DMA
    shapes = (
        jax.ShapeDtypeStruct((1, 1), F32),
        jax.ShapeDtypeStruct((width, voc), BF16),
        jax.ShapeDtypeStruct((2, width), F32),
    )
    results = pl.pallas_call(
        fused,
        out_shape=shapes,
        in_specs=[hbm] * 6,
        out_specs=(hbm, hbm, hbm),
        scratch_shapes=[
            pltpu.VMEM((1, 1), F32),
            pltpu.VMEM((2, width), F32),
            pltpu.VMEM((voc // TAG, TAG), F32),
            pltpu.VMEM((1, TOK), jnp.int32),
            pltpu.VMEM((1, TOK), jnp.int32),
            pltpu.VMEM((1, 32), jnp.int32),
            pltpu.VMEM((width, voc), BF16),
            pltpu.VMEM((2, GROUPS // 2, 4, TOK, width // 4), BF16),
            pltpu.VMEM((2, GROUPS // 2, TOK, TAG), BF16),
            pltpu.VMEM((2, half, voc), BF16),
            pltpu.VMEM((half, voc), BF16),
            pltpu.VMEM((tokens, voc), F32),
            pltpu.VMEM((tokens, voc), F32),
            pltpu.VMEM((tokens, voc), F32),
            pltpu.VMEM((tokens, 3 * TAG), BF16),
            pltpu.VMEM((tokens, voc), BF16),
            pltpu.VMEM((4, 4, TOK, voc), BF16),
            pltpu.VMEM((4, 4, TOK, voc), BF16),
            pltpu.VMEM((6 * TAG, voc), BF16),
            pltpu.VMEM((TAG, voc), F32),
            pltpu.VMEM((PAIR, 16, TAG), F32),
            pltpu.VMEM((PAIR, 16, TAG), F32),
            pltpu.VMEM((4 * TOK, half), F32),
            pltpu.VMEM((4, 4, TOK, half), BF16),
            pltpu.VMEM((4, 4, TOK, half // 4), BF16),
            pltpu.VMEM((4, 4, TOK, half // 4), BF16),
            pltpu.VMEM((4, 4, TOK, half // 4), BF16),
            pltpu.VMEM((2, 4, TOK, half // 2), BF16),
            pltpu.VMEM((6, TOK, half // 2), BF16),
            pltpu.VMEM((2, PAIR, 16, half // 16), BF16),
            pltpu.VMEM((2, PAIR, 16, half // 16), BF16),
            dma((13,)),
            dma,
            dma((32,)),
            dma,
            dma((8,)),
            dma((2,)),
            dma((8,)),
            dma((5,)),
            dma((5,)),
            dma,
            dma,
            dma,
            dma,
            dma,
            dma((12,)),
            dma,
            dma((2,)),
            dma,
            dma((2,)),
        ],
        compiler_params=pltpu.CompilerParams(
            collective_id=0, has_side_effects=True, vmem_limit_bytes=60 * 1024 * 1024
        ),
        name="splade_head",
    )(
        hidden,
        head_weight,
        vocab_bias.reshape(voc // TAG, TAG),
        seq_ids,
        token_mask,
        labels.reshape(1, labels.shape[0]),
    )
    loss, weight_grad, hidden_grad = pl.pallas_call(
        finish,
        out_shape=shapes,
        in_specs=[hbm] * 3,
        out_specs=(hbm,) * 3,
        scratch_shapes=[
            *(pltpu.VMEM(shape.shape, shape.dtype) for shape in shapes),
            dma((CHUNKS + 2,)),
            dma((CHUNKS + 2,)),
        ],
        compiler_params=pltpu.CompilerParams(vmem_limit_bytes=60 * 1024 * 1024),
        name="results",
    )(*results)
    return loss.reshape(()), weight_grad, hidden_grad


def solution(mesh):
    in_specs = (
        P("dp", None),
        P(None, ("dp", "vocab")),
        P(("dp", "vocab")),
        P("dp", None),
        P("dp", None),
        P(),
    )
    out_specs = (P(), P(None, ("dp", "vocab")), P(("dp", "vocab"), None))
    return jax.shard_map(body, mesh=mesh, in_specs=in_specs, out_specs=out_specs, check_vma=False)
```
